32 devices in a mesh: dp: 8 (over z, y), ctx: 4 (over x, core).
Axes of the slice: x: 2, y: 2, z: 4, core: 2. Of those that a mesh axis runs over, the one named last changes fastest.
Arguments:
- queries: bfloat16 [8, 512, 16, 128], P('dp', 'ctx'), may hold values from -6 to 6
- keys: bfloat16 [8, 512, 16, 128], P('dp', 'ctx'), may hold values from -6 to 6
- values: bfloat16 [8, 512, 16, 128], P('dp', 'ctx'), may hold values from -6 to 6
- out_grad: bfloat16 [8, 512, 16, 128], P('dp', 'ctx'), may hold values from -0.59765625 to 0.59765625
- gate_weight: bfloat16 [16, 128], P(None, 'dp'), may hold values from -0.5 to 0.5
- head_bias: bfloat16 [16], replicated, as said below
Outputs:
- query_grad: bfloat16 [8, 512, 16, 128], P('dp', 'ctx')
- key_grad: bfloat16 [8, 512, 16, 128], P('dp', 'ctx')
- gate_grad: float32 [16, 128], P(None, 'dp')
The draws below stay inside these ranges and needn't reach their ends.
Inputs may be any that keep to these rules, and one draw needn't show every extreme that they name: `head_bias`: each entry lies between -ln(512) - 1.5 and -3.5.
All inputs are finite; a program needn't handle non-finite values.
Results may differ from the reference program's by a relative error of at most 0.0038.
The reference program's roundings to bfloat16 on the way count: a program that leaves them out, or rounds other values in their place, can miss the bound.
Values may be sent and summed in bfloat16 or wider, within the bound.
No kernel may reach another device: no remote copies, remote signals or barrier semaphores. Data moves between devices by JAX's collectives and lax.ppermute only.
A program may use at most 128 MiB of HBM per device.

```python
import jax
import jax.numpy as jnp
from jax import lax

H = 16
HD = 128
TOK_DEV = 128
LENGTH = 512
HISTS = 8


def draw_head_bias(key, part):
    first, second, third = jax.random.split(jax.random.fold_in(key, 17), 3)
    share = 0.5
    quick = jax.random.uniform(first, (H,)) < share
    slow = -jnp.log(jnp.float32(LENGTH)) + jax.random.uniform(second, (H,), jnp.float32, -1.5, 0.0)
    fast = jax.random.uniform(third, (H,), jnp.float32, -4.8, -3.6)
    return jnp.where(quick, fast, slow).astype(jnp.bfloat16)


def level_of(rng, shape, cuts, low, largest):
    def one(axis_at, blocks):
        steps = jax.random.uniform(jax.random.fold_in(jax.random.fold_in(rng, 6), axis_at), (blocks,), jnp.float32, low / len(cuts), largest / len(cuts))
        return jnp.repeat(jnp.exp(steps), shape[axis_at] // blocks).reshape((-1,) + (1,) * (len(shape) - axis_at - 1))

    factor_of = one(*cuts[0])
    for cut in cuts[1:]:
        factor_of = factor_of * one(*cut)
    return factor_of


def centred(stream_key, extent, scale, limit, cuts=(), held_as=jnp.bfloat16):
    drawn = scale * jax.random.normal(stream_key, extent, jnp.float32)
    if cuts:
        drawn = drawn * level_of(stream_key, extent, cuts, -0.22, 0.18)
    return jnp.clip(drawn, -limit, limit).astype(held_as)


def setup_inputs(seed: int = 0) -> dict:
    key_list = jax.random.split(jax.random.key(seed), 7)
    queries = centred(key_list[0], (HISTS, LENGTH, H, HD), 1.0, 6.0, ((0, 8), (1, 4)))
    keys = centred(key_list[1], (HISTS, LENGTH, H, HD), 1.0, 6.0, ((0, 8), (1, 4)))
    values = centred(key_list[2], (HISTS, LENGTH, H, HD), 1.0, 6.0, ((0, 8), (1, 4)))
    out_grad = centred(key_list[3], (HISTS, LENGTH, H, HD), 0.088, 0.59765625, ((0, 8), (1, 4)))
    gate_weight = centred(key_list[4], (H, HD), HD ** -0.5, 0.5, ((1, 8),))
    head_bias = draw_head_bias(jax.random.fold_in(key_list[6], 71), 0)
    return dict(queries=queries, keys=keys, values=values, out_grad=out_grad, gate_weight=gate_weight, head_bias=head_bias)


def gate_logit(keys_block, gate_rows, bias_rows):
    return jnp.sum(keys_block.astype(jnp.float32) * gate_rows.astype(jnp.float32)[None], -1) + bias_rows.astype(jnp.float32)[None]


def key_state(keys_block, values_block, cumul):
    tail = jnp.exp(cumul[-1][None] - cumul)[:, :, None]
    scaled = (keys_block.astype(jnp.float32) * tail).astype(jnp.bfloat16)
    return jnp.exp(cumul[-1]), jnp.einsum('chd,che->hde', scaled, values_block, preferred_element_type=jnp.float32)


def query_state(queries_block, grads_block, cumul):
    head = jnp.exp(cumul)[:, :, None]
    scaled = (queries_block.astype(jnp.float32) * head).astype(jnp.bfloat16)
    return jnp.exp(cumul[-1]), jnp.einsum('chd,che->hde', scaled, grads_block, preferred_element_type=jnp.float32)


def block_grads(queries_block, keys_block, values_block, grads_block, cumul, incoming, outgoing, scale):
    count = queries_block.shape[0]
    rows = lax.broadcasted_iota(jnp.int32, (count, count), 0)
    cols = lax.broadcasted_iota(jnp.int32, (count, count), 1)
    causal = rows >= cols
    trans = cumul.T
    gap = trans[:, :, None] - trans[:, None, :]
    decay = jnp.exp(jnp.where(causal[None], gap, -1e30))
    products = jnp.einsum('the,she->hts', grads_block, values_block, preferred_element_type=jnp.float32)
    wround = (scale * products * decay).astype(jnp.bfloat16)
    head = jnp.exp(cumul)[:, :, None]
    tail = jnp.exp(cumul[-1][None] - cumul)[:, :, None]
    in_round = incoming.astype(jnp.bfloat16)
    out_round = outgoing.astype(jnp.bfloat16)
    qgrad = jnp.einsum('hts,shd->thd', wround, keys_block, preferred_element_type=jnp.float32) + scale * head * jnp.einsum('the,hde->thd', grads_block, in_round, preferred_element_type=jnp.float32)
    kgrad = jnp.einsum('hts,thd->shd', wround, queries_block, preferred_element_type=jnp.float32) + scale * tail * jnp.einsum('she,hde->shd', values_block, out_round, preferred_element_type=jnp.float32)
    dgsum = jnp.sum(queries_block.astype(jnp.float32) * qgrad, -1) - jnp.sum(keys_block.astype(jnp.float32) * kgrad, -1)
    return qgrad, kgrad, dgsum


def finish(qgrad, kgrad, dgsum, after, logit, keys_block, gate_rows):
    total = after[None] + jnp.sum(dgsum, 0)[None] - jnp.cumsum(dgsum, 0) + dgsum
    dlogit = -jax.nn.sigmoid(logit) * total
    rounded = lax.optimization_barrier(kgrad.astype(jnp.bfloat16)).astype(jnp.float32)
    key_out = (rounded + dlogit[:, :, None] * gate_rows.astype(jnp.float32)[None]).astype(jnp.bfloat16)
    weight_term = jnp.sum(dlogit[:, :, None] * keys_block.astype(jnp.float32), 0)
    return qgrad.astype(jnp.bfloat16), key_out, weight_term


def sequence_grads(queries_seq, keys_seq, values_seq, grads_seq, gate_rows, bias_rows, block):
    length, heads, width = queries_seq.shape
    count = length // block
    scale = 1.0 / width
    logit = gate_logit(keys_seq, gate_rows, bias_rows)
    cumul = jnp.cumsum(-jax.nn.softplus(logit).reshape(count, block, heads), axis=1)
    logit_blocks = logit.reshape(count, block, heads)

    def split(array):
        return array.reshape(count, block, heads, width)

    qb, kb, vb, gb = split(queries_seq), split(keys_seq), split(values_seq), split(grads_seq)
    zeros = jnp.zeros((heads, width, width), jnp.float32)

    def forward(state, items):
        kx, vx, cx = items
        factor, update = key_state(kx, vx, cx)
        return factor[:, None, None] * state + update, state

    _, incoming = lax.scan(forward, zeros, (kb, vb, cumul))

    def backward(carry, items):
        outgoing, after, accum = carry
        qx, kx, vx, gx, cx, sx, lx = items
        factor, update = query_state(qx, gx, cx)
        qgrad, kgrad, dgsum = block_grads(qx, kx, vx, gx, cx, sx, outgoing, scale)
        qout, kout, term = finish(qgrad, kgrad, dgsum, after, lx, kx, gate_rows)
        return (factor[:, None, None] * outgoing + update, after + jnp.sum(dgsum, 0), accum + term), (qout, kout)

    start = (zeros, jnp.zeros((heads,), jnp.float32), jnp.zeros((heads, width), jnp.float32))
    (_, _, accum), (qouts, kouts) = lax.scan(backward, start, (qb, kb, vb, gb, cumul, incoming, logit_blocks), reverse=True)
    return qouts.reshape(length, heads, width), kouts.reshape(length, heads, width), accum


def reference(queries, keys, values, out_grad, gate_weight, head_bias):
    def single(items):
        qx, kx, vx, gx = items
        return sequence_grads(qx, kx, vx, gx, gate_weight, head_bias, TOK_DEV)

    query_grad, key_grad, terms = lax.map(single, (queries, keys, values, out_grad))
    return query_grad, key_grad, jnp.sum(terms, 0)
```

```python
import functools

import jax
import jax.numpy as jnp
from jax import lax
from jax.experimental import pallas as pl
from jax.experimental.pallas import tpu as pltpu
from jax.sharding import PartitionSpec as P

F32 = jnp.float32
BF16 = jnp.bfloat16
VMEM = pl.BlockSpec(memory_space=pltpu.VMEM)
ANY = pl.BlockSpec(memory_space=pl.ANY)
LIMIT = 24 * 1024 * 1024


def nn(a, b):
    return lax.dot_general(a, b, (((1,), (0,)), ((), ())), preferred_element_type=F32)


def nt(a, b):
    return lax.dot_general(a, b, (((1,), (1,)), ((), ())), preferred_element_type=F32)


def place():
    mine = lax.axis_index("ctx")
    return lax.rem(mine, 2), lax.div(mine, 2)


def hi_lo(rows):
    hi = rows.astype(BF16)
    return hi, (rows - hi.astype(F32)).astype(BF16)


def params(**more):
    return pltpu.CompilerParams(vmem_limit_bytes=LIMIT, **more)


def split_kernel(k_ref, q_ref, v_ref, g_ref, keep_ref, send_ref, tmp):
    par, _ = place()
    _, count, heads, width = k_ref.shape
    half = heads // 2
    for at, ref in enumerate((k_ref, q_ref, v_ref, g_ref)):
        tmp[...] = ref[0].astype(F32).reshape(count * heads, width)
        for j in range(half):
            for out, base in ((keep_ref, par * half), (send_ref, (1 - par) * half)):
                plane = tmp[pl.ds(base + j, count, stride=heads), :]
                if at < 2:
                    plane = plane.T
                out[at, j] = plane.astype(BF16)


def load_both(keep_ref, recv_ref, buf, sems, par):
    copies = []
    for at in range(4):
        pair = (
            pltpu.make_async_copy(keep_ref.at[at], buf.at[par, at], sems.at[0, at]),
            pltpu.make_async_copy(recv_ref.at[at], buf.at[1 - par, at], sems.at[1, at]),
        )
        for copy in pair:
            copy.start()
        copies.append(pair)
    return copies


def scales(rows):
    end = jnp.broadcast_to(rows[:, -1:], rows.shape)
    return jnp.exp(end - rows), jnp.exp(rows), jnp.exp(end)


def state(buf, scale_ref, side, block, j):
    half = buf.shape[2]
    scaled = buf[block, side, j].astype(F32) * scale_ref[side, pl.ds(block * half + j, 1), :]
    return nn(scaled.astype(BF16), buf[block, 2 + side, j])


def gate_kernel(direct, pair, *refs):
    if direct:
        mine_ref, other_ref = refs[:2]
        refs = refs[2:]
    else:
        full_ref = refs[0]
        refs = refs[1:]
    bias_ref, keep_ref, recv_ref, total_ref, near_ref, rows_ref, gate_ref, buf, scale_ref, sems = refs
    par, chip = place()
    half, width, count = buf.shape[2:]
    copies = load_both(keep_ref, recv_ref, buf, sems, par)
    if direct:
        index = lax.axis_index("dp")
        pieces, _, piece = mine_ref.shape
        sub = lax.broadcasted_iota(jnp.int32, (piece, width), 0)
        lane = lax.broadcasted_iota(jnp.int32, (piece, width), 1)
        full = jnp.zeros((2 * half, width), F32)
        for ref, low in ((mine_ref, par), (other_ref, 1 - par)):
            for k in range(pieces):
                owner = jnp.bitwise_xor(index, 2 * k + low)
                pick = jnp.where(lane == sub + owner * piece, 1.0, 0.0).astype(BF16)
                full = full + nn(ref[k], pick)
    else:
        full = full_ref[...].astype(F32)
    gate_ref[...] = full
    weights = gate_ref[pl.ds(par * half, half), :].astype(BF16)
    bias = bias_ref[pl.ds(par * half, half), :]
    row = lax.broadcasted_iota(jnp.int32, (half, count), 0)
    for copy in copies[0]:
        copy.wait()
    logits = []
    for block in range(2):
        logit = bias
        for j in range(half):
            logit = logit + jnp.where(row == j, nn(weights, buf[block, 0, j]), 0.0)
        logits.append(logit)
    logit = jnp.concatenate(logits, 0)
    decay = -(jnp.maximum(logit, 0.0) + jnp.log1p(jnp.exp(-jnp.abs(logit))))
    until = lax.broadcasted_iota(jnp.int32, (count, count), 0) <= lax.broadcasted_iota(jnp.int32, (count, count), 1)
    cumul = lax.dot_general(
        decay,
        jnp.where(until, 1.0, 0.0),
        (((1,), (0,)), ((), ())),
        precision=lax.Precision.HIGHEST,
        preferred_element_type=F32,
    )
    rows_ref[0] = cumul
    rows_ref[1] = -1.0 / (1.0 + jnp.exp(-logit))
    tail, head, ends = scales(cumul)
    scale_ref[0] = tail
    scale_ref[1] = head
    scale_ref[2] = ends
    for at in (1, 2, 3):
        for copy in copies[at]:
            copy.wait()
    for at, side in enumerate((chip,) if pair else (0, 1)):
        for j in range(half):
            near = state(buf, scale_ref, side, side, j)
            last = state(buf, scale_ref, side, 1 - side, j)
            passed = scale_ref[2, pl.ds((1 - side) * half + j, 1), :] * near + last
            total_ref[at, j] = passed.astype(total_ref.dtype)
            near_ref[at, j] = near.astype(near_ref.dtype)


def put(out, buf, mine_ref, send_ref, at, side, rel, block, j, full):
    rounded = full.astype(BF16)
    (mine_ref if rel == 0 else send_ref)[at, j] = rounded.astype(F32).T.astype(BF16)
    sign = jnp.where(side == 0, 1.0, -1.0)
    out.append(sign * jnp.sum(buf[block, 1 - side, j].astype(F32) * full, 0, keepdims=True))


def weighted_keys(buf, block, rows):
    half = buf.shape[2]
    lhs = jnp.concatenate(hi_lo(rows), 0)
    row = lax.broadcasted_iota(jnp.int32, lhs.shape, 0)
    total = jnp.zeros(lhs.shape, F32)
    for j in range(half):
        total = total + jnp.where((row == j) | (row == j + half), nt(lhs, buf[block, 0, j]), 0.0)
    return total[:half] + total[half:]


def inside_kernel(pair, keep_ref, recv_ref, rows_ref, near_ref, *refs):
    if pair:
        attn_ref, kappa_ref, other_ref, mine_ref, send_ref, dg_ref, buf, scale_ref, sems = refs
    else:
        attn_ref, kappa_ref, buf, scale_ref, sems = refs
    par, chip = place()
    half, width, count = buf.shape[2:]
    const = 1.0 / width
    copies = load_both(keep_ref, recv_ref, buf, sems, par)
    cumul = rows_ref[0]
    columns = cumul.T
    tail, head, ends = scales(cumul)
    scale_ref[0] = tail
    scale_ref[1] = head
    causal = lax.broadcasted_iota(jnp.int32, (count, count), 0) >= lax.broadcasted_iota(jnp.int32, (count, count), 1)
    for loaded in copies:
        for copy in loaded:
            copy.wait()
    kappa = jnp.zeros((half, width), F32)
    for block in range(2):
        kappa = kappa + weighted_keys(buf, block, rows_ref[1, pl.ds(block * half, half), :])
    kappa_ref[...] = kappa
    if pair:
        side = chip
        for j in range(half):
            other_ref[j] = state(buf, scale_ref, 1 - side, 1 - side, j)
    sums = [[], []]
    for rel in range(2):
        block = par if rel == 0 else 1 - par
        for j in range(half):
            at = pl.ds(block * half + j, 1)
            line = rows_ref[0, at, :]
            column = jnp.where(par == rel, columns[:, j : j + 1], columns[:, half + j : half + j + 1])
            decay = jnp.exp(jnp.where(causal, column - line, -1e30))
            weight = (const * nt(buf[block, 3, j], buf[block, 2, j]) * decay).astype(BF16)
            query = nt(buf[block, 0, j], weight)
            key = nn(buf[block, 1, j], weight)
            if pair:
                known = jnp.where(side == 0, query, key)
                attn_ref[0, rel, j] = jnp.where(side == 0, key, query)
                cross = nt(near_ref[0, j], buf[block, 3 - side, j])
                factor = jnp.where(block == side, 0.0, const) * scale_ref[1 - side, at, :]
                put(sums[rel], buf, mine_ref, send_ref, 0, side, rel, block, j, known + factor * cross)
            else:
                attn_ref[0, rel, j] = query
                attn_ref[1, rel, j] = key
    if pair:
        for rel in range(2):
            dg_ref[rel] = jnp.concatenate(sums[rel], 0)
            send_rows = jnp.concatenate(
                hi_lo(rows_ref[1, pl.ds((1 - par) * half, half), :]), 0
            )
        send_ref[0, half, : 2 * half] = send_rows


def outside_kernel(pair, keep_ref, recv_ref, rows_ref, state_ref, near_ref, attn_ref, kappa_ref, *refs):
    if pair:
        dg_ref, mine_ref, send_ref, suffix_ref, pieces_ref, buf, scale_ref, sems = refs
    else:
        mine_ref, send_ref, suffix_ref, pieces_ref, buf, scale_ref, sems = refs
    par, chip = place()
    half, width, count = buf.shape[2:]
    const = 1.0 / width
    copies = load_both(keep_ref, recv_ref, buf, sems, par)
    cumul = rows_ref[0]
    tail, head, ends = scales(cumul)
    scale_ref[0] = tail
    scale_ref[1] = head
    scale_ref[2] = ends
    for loaded in copies:
        for copy in loaded:
            copy.wait()
    if pair:
        slopes = [dg_ref[0], dg_ref[1]]
        sides = (1 - chip,)
    else:
        slopes = [jnp.zeros((half, count), F32)] * 2
        sides = (0, 1)
    for rel in range(2):
        block = par if rel == 0 else 1 - par
        for at, side in enumerate(sides):
            sums = []
            for j in range(half):
                entry = block == side
                come = state_ref[at, j].astype(F32)
                ratio = jnp.where(entry, 1.0, scale_ref[2, pl.ds(side * half + j, 1), :])
                near = near_ref[j] if pair else near_ref[at, j]
                known = (ratio * come + jnp.where(entry, 0.0, 1.0) * near).astype(BF16)
                cross = nt(known, buf[block, 3 - side, j])
                factor = const * scale_ref[1 - side, pl.ds(block * half + j, 1), :]
                full = attn_ref[at, rel, j] + factor * cross
                put(sums, buf, mine_ref, send_ref, at, side, rel, block, j, full)
            slopes[rel] = slopes[rel] + jnp.concatenate(sums, 0)
    slope = jnp.concatenate(slopes, 0)
    later = lax.broadcasted_iota(jnp.int32, (count, count), 0) >= lax.broadcasted_iota(jnp.int32, (count, count), 1)
    suffix = lax.dot_general(
        slope,
        jnp.where(later, 1.0, 0.0),
        (((1,), (0,)), ((), ())),
        precision=lax.Precision.HIGHEST,
        preferred_element_type=F32,
    )
    sums = jnp.broadcast_to(suffix[:, :1], suffix.shape)
    first = (par == 0).astype(F32)
    mine = suffix[:half] + first * sums[half:]
    other = suffix[half:] + (1.0 - first) * sums[:half]
    suffix_ref[0] = mine
    suffix_ref[1] = rows_ref[1, pl.ds(par * half, half), :]
    last = send_ref.shape[0] - 1
    send_ref[last, half, : 2 * half] = jnp.concatenate(hi_lo(other), 0)
    if not pair:
        send_ref[0, half, : 2 * half] = jnp.concatenate(
            hi_lo(rows_ref[1, pl.ds((1 - par) * half, half), :]), 0
        )
    partial = weighted_keys(buf, par, mine * rows_ref[1, pl.ds(par * half, half), :])
    partial = partial + weighted_keys(buf, 1 - par, other * rows_ref[1, pl.ds((1 - par) * half, half), :])
    kappa = kappa_ref[...]
    total = sums[:half] + sums[half:]
    parts = lax.axis_size("dp")
    copies_of = pieces_ref.shape[0] // parts
    piece = width // parts
    lane = lax.broadcasted_iota(jnp.int32, (half, width), 1)
    for i in range(parts):
        gates = partial if i == 0 else pltpu.roll(partial, width - i * piece, 1)
        shift = (width - i * piece + piece) % width
        slopes_of = kappa if shift == 0 else pltpu.roll(kappa, shift, 1)
        sent = jnp.where(lane < piece, gates, jnp.where(lane < 2 * piece, slopes_of, total))
        pieces_ref[pl.ds(i * copies_of, copies_of)] = jnp.broadcast_to(sent[None], (copies_of, half, width))


def last_kernel(pair, mine_refs, recv_refs, suffix_ref, pieces_ref, gate_ref, refs):
    query_ref, key_ref, grad_ref, buf, tmp, line_ref, sems = refs
    par, chip = place()
    index = lax.axis_index("dp")
    half = suffix_ref.shape[1]
    _, count, heads, width = query_ref.shape
    parts, ranks = lax.axis_size("dp"), lax.axis_size("ctx")
    piece = width // parts

    def copies(side):
        local = pair and (lambda source: source)
        del local
        return None

    def start(side, source_mine, source_recv):
        pltpu.make_async_copy(source_mine, buf.at[side, par, pl.ds(0, half)], sems.at[side, 0]).start()
        pltpu.make_async_copy(source_recv, buf.at[side, 1 - par], sems.at[side, 1]).start()

    if pair:
        for side in range(2):

            @pl.when(chip == side)
            def _(side=side):
                start(side, mine_refs[0].at[0], recv_refs[0].at[0])

            @pl.when(chip != side)
            def _(side=side):
                start(side, mine_refs[1].at[0], recv_refs[1].at[0])
    else:
        for side in range(2):
            start(side, mine_refs[0].at[side], recv_refs[0].at[side])

    def wait(side):
        source_mine = mine_refs[0].at[0]
        source_recv = recv_refs[0].at[0]
        pltpu.make_async_copy(source_mine, buf.at[side, par, pl.ds(0, half)], sems.at[side, 0]).wait()
        pltpu.make_async_copy(source_recv, buf.at[side, 1 - par], sems.at[side, 1]).wait()

    groups = ranks // 2
    total = jnp.zeros((2, half, width), F32)
    everything = pieces_ref[...].reshape(parts, groups, 2, half, width)
    after = jnp.zeros((parts, 2, half, 1), F32)
    for m in reversed(range(groups)):
        got = everything[:, m]
        slopes = pltpu.roll(got.reshape(parts * 2 * half, width), width - piece, 1).reshape(got.shape)
        total = total + jnp.sum(got + slopes * after, 0)
        after = after + got[..., 2 * piece : 2 * piece + 1]
    grad_ref[...] = total.reshape(heads, width)[:, :piece]

    own = pieces_ref[pl.ds(index * ranks, ranks)].reshape(groups, 2, half, width)
    beyond = jnp.zeros((2, half, 1), F32)
    for m in range(groups):
        beyond = beyond + jnp.where(m > chip, 1.0, 0.0) * own[m, :, :, 2 * piece : 2 * piece + 1]

    wait(0)
    wait(1)
    for side, ref in ((0, query_ref), (1, key_ref)):
        if side == 1:
            local, remote = (chip, 1 - chip) if pair else (0, 1)
            slope_rows = buf[local, 1 - par, half, : 2 * half].astype(F32)
            suffix_rows = buf[remote, 1 - par, half, : 2 * half].astype(F32)
            line_ref[0, pl.ds(par * half, half), :] = suffix_ref[0]
            line_ref[0, pl.ds((1 - par) * half, half), :] = suffix_rows[:half] + suffix_rows[half:]
            line_ref[1, pl.ds(par * half, half), :] = suffix_ref[1]
            line_ref[1, pl.ds((1 - par) * half, half), :] = slope_rows[:half] + slope_rows[half:]
            slope = line_ref[1] * (line_ref[0] + beyond.reshape(heads, 1))
            columns = slope.T
        for h in range(heads):
            plane = buf[side, h // half, h % half].astype(F32)
            if side == 1:
                plane = plane + columns[:, h : h + 1] * gate_ref[h : h + 1, :]
            tmp[side, pl.ds(h, count, stride=heads), :] = plane
        ref[0] = tmp[side].reshape(count, heads, width).astype(BF16)


def across_chips(total, ends, ranks, reverse):
    step = -1 if reverse else 1

    def shift(value, chips):
        hops = [(i, i + 2 * chips * step) for i in range(ranks) if 0 <= i + 2 * chips * step < ranks]
        return lax.ppermute(value, "ctx", hops)

    value, factor = shift(total, 1), shift(ends, 1)
    reach = 1
    while 2 * reach < ranks:
        value = value + factor * shift(value, reach)
        factor = factor * shift(factor, reach)
        reach *= 2
    return value


def per_device(mesh, queries, keys, values, out_grad, gate_weight, head_bias):
    _, count, heads, width = queries.shape
    parts, ranks = mesh.shape["dp"], mesh.shape["ctx"]
    half = heads // 2
    pair = ranks == 4
    direct = parts == 8
    swap = [(i, i ^ 1) for i in range(ranks)]
    plane = (half, width, count)

    if direct:
        got = []
        for k in range(parts // 2):
            hops = [
                (d * ranks + c, (d ^ (2 * k + c % 2)) * ranks + c)
                for d in range(parts)
                for c in range(ranks)
            ]
            got.append(lax.ppermute(gate_weight, ("dp", "ctx"), hops))
        mine_gate = jnp.stack(got)
        gates = (mine_gate, lax.ppermute(mine_gate, "ctx", swap))
    else:
        gates = (lax.all_gather(gate_weight, "dp", axis=1, tiled=True),)
    bias = jnp.broadcast_to(head_bias.astype(F32)[:, None], (heads, count))

    quad = jax.ShapeDtypeStruct((4, *plane), BF16)
    keep, send = pl.pallas_call(
        split_kernel,
        out_shape=(quad, quad),
        in_specs=[VMEM] * 4,
        out_specs=(VMEM, VMEM),
        scratch_shapes=[pltpu.VMEM((count * heads, width), F32)],
        compiler_params=params(),
        name="split_heads",
    )(keys, queries, values, out_grad)
    recv = lax.ppermute(send, "ctx", swap)

    buffers = [
        pltpu.VMEM((2, 4, *plane), BF16),
        pltpu.VMEM((3, heads, count), F32),
        pltpu.SemaphoreType.DMA((2, 4)),
    ]
    sides = 1 if pair else 2
    square = (half, width, width)
    total, near, rows, gate_full = pl.pallas_call(
        functools.partial(gate_kernel, direct, pair),
        out_shape=(
            jax.ShapeDtypeStruct((sides, *square), BF16 if pair else F32),
            jax.ShapeDtypeStruct((sides, *square), BF16 if pair else F32),
            jax.ShapeDtypeStruct((2, heads, count), F32),
            jax.ShapeDtypeStruct((heads, width), F32),
        ),
        in_specs=[VMEM] * (len(gates) + 1) + [ANY, ANY],
        out_specs=(VMEM,) * 4,
        scratch_shapes=buffers,
        compiler_params=params(),
        name="gate_states",
    )(*gates, bias, keep, recv)

    attn_shape = jax.ShapeDtypeStruct((sides, 2, *plane), F32)
    kappa_shape = jax.ShapeDtypeStruct((half, width), F32)
    mine_shape = jax.ShapeDtypeStruct((sides, half, count, width), BF16)
    send_shape = jax.ShapeDtypeStruct((sides, half + 1, count, width), BF16)
    slope_shape = jax.ShapeDtypeStruct((2, half, count), F32)
    pieces_shape = jax.ShapeDtypeStruct((parts * ranks, half, width), F32)
    inside = pl.pallas_call(
        functools.partial(inside_kernel, pair),
        out_shape=(attn_shape, kappa_shape)
        + ((jax.ShapeDtypeStruct(square, F32), mine_shape, send_shape, slope_shape) if pair else ()),
        in_specs=[ANY, ANY, VMEM, VMEM],
        out_specs=(VMEM,) * (6 if pair else 2),
        scratch_shapes=buffers,
        compiler_params=params(),
        name="inside_block",
    )
    if pair:
        states = lax.ppermute(total, "ctx", [(i, i ^ 2) for i in range(ranks)])
        attn, kappa, near, mine_local, send_local, slopes = inside(keep, recv, rows, near)
        recv_local = lax.ppermute(send_local, "ctx", swap)
        extra = (slopes,)
    else:
        ends = jnp.exp(rows[0, :half, -1] + rows[0, half:, -1])[:, None, None]
        states = jnp.stack(
            [across_chips(total[0], ends, ranks, False), across_chips(total[1], ends, ranks, True)]
        )
        attn, kappa = inside(keep, recv, rows, near)
        extra = ()
    mine, send, suffix, pieces = pl.pallas_call(
        functools.partial(outside_kernel, pair),
        out_shape=(mine_shape, send_shape, slope_shape, pieces_shape),
        in_specs=[ANY, ANY] + [VMEM] * (5 + len(extra)),
        out_specs=(VMEM,) * 4,
        scratch_shapes=buffers,
        compiler_params=params(),
        name="outside_block",
    )(keep, recv, rows, states, near, attn, kappa, *extra)
    recv_out = lax.ppermute(send, "ctx", swap)
    pieces = lax.all_to_all(pieces, ("dp", "ctx"), 0, 0, tiled=True)

    mines = (mine_local, mine) if pair else (mine,)
    recvs = (recv_local, recv_out) if pair else (recv_out,)

    def last(*refs):
        n = len(mines)
        last_kernel(pair, refs[:n], refs[n : 2 * n], *refs[2 * n : 2 * n + 3], refs[2 * n + 3 :])

    piece = width // parts
    return pl.pallas_call(
        last,
        out_shape=(
            jax.ShapeDtypeStruct((1, count, heads, width), BF16),
            jax.ShapeDtypeStruct((1, count, heads, width), BF16),
            jax.ShapeDtypeStruct((heads, piece), F32),
        ),
        in_specs=[ANY] * (2 * len(mines)) + [VMEM] * 3,
        out_specs=(VMEM,) * 3,
        scratch_shapes=[
            pltpu.VMEM((2, 2, half + 1, count, width), BF16),
            pltpu.VMEM((2, count * heads, width), F32),
            pltpu.VMEM((2, heads, count), F32),
            pltpu.SemaphoreType.DMA((2, 2)),
        ],
        compiler_params=params(),
        name="last",
    )(*mines, *recvs, suffix, pieces, gate_full)


def solution(mesh):
    return jax.shard_map(
        functools.partial(per_device, mesh),
        mesh=mesh,
        in_specs=(
            P("dp", "ctx", None, None),
            P("dp", "ctx", None, None),
            P("dp", "ctx", None, None),
            P("dp", "ctx", None, None),
            P(None, "dp"),
            P(),
        ),
        out_specs=(P("dp", "ctx", None, None), P("dp", "ctx", None, None), P(None, "dp")),
        check_vma=False,
    )
```

```python
import functools

import jax
import jax.numpy as jnp
from jax import lax
from jax.experimental import pallas as pl
from jax.experimental.pallas import tpu as pltpu
from jax.sharding import PartitionSpec as P

F32 = jnp.float32
BF16 = jnp.bfloat16
VMEM = pl.BlockSpec(memory_space=pltpu.VMEM)
ANY = pl.BlockSpec(memory_space=pl.ANY)
HBM = pl.BlockSpec(memory_space=pltpu.HBM)
LIMIT = 24 * 1024 * 1024


def nn(a, b):
    return lax.dot_general(a, b, (((1,), (0,)), ((), ())), preferred_element_type=F32)


def nt(a, b):
    return lax.dot_general(a, b, (((1,), (1,)), ((), ())), preferred_element_type=F32)


def exact(a, b):
    return lax.dot_general(
        a, b, (((1,), (0,)), ((), ())), precision=lax.Precision.HIGHEST, preferred_element_type=F32
    )


def iota(shape, dim):
    return lax.broadcasted_iota(jnp.int32, shape, dim)


def place():
    mine = lax.axis_index("ctx")
    return lax.rem(mine, 2), lax.div(mine, 2)


def hi_lo(rows):
    hi = rows.astype(BF16)
    return jnp.concatenate([hi, (rows - hi.astype(F32)).astype(BF16)], 0)


def call(kernel, name, out_shape, operands, scratch=(), micros=1.0, in_specs=None, out_specs=None, limit=LIMIT):
    outs = len(out_shape)
    return pl.pallas_call(
        kernel,
        out_shape=out_shape,
        in_specs=in_specs or [VMEM] * len(operands),
        out_specs=out_specs or (VMEM,) * outs,
        scratch_shapes=list(scratch),
        compiler_params=pltpu.CompilerParams(vmem_limit_bytes=limit),
        cost_estimate=pl.CostEstimate(
            flops=0, bytes_accessed=int(micros * 3_000_000), transcendentals=0
        ),
        name=name,
    )(*operands)


def split_kernel(k_ref, q_ref, v_ref, g_ref, keep_ref, send_ref, buf, planes, sems, out_sems):
    par, _ = place()
    _, count, heads, width = k_ref.shape
    half = heads // 2
    loads = [
        pltpu.make_async_copy(ref.at[0], buf.at[at], sems.at[at])
        for at, ref in enumerate((k_ref, q_ref, v_ref, g_ref))
    ]
    for load in loads:
        load.start()
    stores = []
    for at, load in enumerate(loads):
        load.wait()
        turned = jnp.swapaxes(buf[at], 0, 1)
        for h in range(heads):
            plane = turned[h]
            planes[at, h // half, h % half] = plane.T if at < 2 else plane
        for out, which, side in ((send_ref, 1 - par, 0), (keep_ref, par, 1)):
            store = pltpu.make_async_copy(planes.at[at, which], out.at[at], out_sems.at[at, side])
            store.start()
            stores.append(store)
    for store in stores:
        store.wait()


def scales(rows):
    end = jnp.broadcast_to(rows[:, -1:], rows.shape)
    return jnp.exp(end - rows), jnp.exp(rows), jnp.exp(end)


def weight_kernel(direct, *refs):
    *gates, bias_ref, gate_ref = refs
    heads, width = gate_ref.shape[1:]
    if direct:
        index = lax.axis_index("dp")
        full = jnp.zeros((heads, width), F32)
        for r, ref in enumerate(gates):
            for low in range(2):
                piece = ref.shape[2]
                owner = jnp.bitwise_xor(index, 2 * r + low)
                pick = iota((piece, width), 1) == iota((piece, width), 0) + owner * piece
                full = full + nn(ref[low], jnp.where(pick, 1.0, 0.0).astype(BF16))
    else:
        full = gates[0][...].astype(F32)
    gate_ref[0] = full
    gate_ref[1] = bias_ref[...]


def gate_kernel(pair, gate_ref, keep_ref, recv_ref, total_ref, near_ref, rows_ref, scale_ref):
    par, chip = place()
    _, half, width, count = keep_ref.shape
    weights = gate_ref[0, pl.ds(par * half, half), :].astype(BF16)
    bias = gate_ref[1, pl.ds(par * half, half), :]
    row = iota((half, count), 0)
    logits = []
    for ref in (keep_ref, recv_ref):
        logit = bias
        for j in range(half):
            logit = logit + jnp.where(row == j, nn(weights, ref[0, j]), 0.0)
        logits.append(logit)
    logit = jnp.concatenate(logits, 0)
    decay = -(jnp.maximum(logit, 0.0) + jnp.log1p(jnp.exp(-jnp.abs(logit))))
    cumul = exact(decay, jnp.where(iota((count, count), 0) <= iota((count, count), 1), 1.0, 0.0))
    rows_ref[0] = cumul
    rows_ref[1] = -1.0 / (1.0 + jnp.exp(-logit))
    tail, head, ends = scales(cumul)
    scale_ref[0] = tail
    scale_ref[1] = head
    for at, side in enumerate((chip,) if pair else (0, 1)):
        enters = par == side
        for j in range(half):
            states = []
            for rel, ref in enumerate((keep_ref, recv_ref)):
                line = scale_ref[side, rel * half + j : rel * half + j + 1, :]
                scaled = (ref[side, j].astype(F32) * line).astype(BF16)
                states.append(nn(scaled, ref[2 + side, j]))
            own, other = states
            passed = (
                jnp.where(enters, ends[half + j : half + j + 1], 1.0) * own
                + jnp.where(enters, 1.0, ends[j : j + 1]) * other
            )
            total_ref[at, j] = passed.astype(total_ref.dtype)
            near_ref[at, j] = jnp.where(enters, own, other).astype(near_ref.dtype)


def weighted_keys(ref, rows):
    half = rows.shape[0]
    lhs = hi_lo(rows)
    row = iota(lhs.shape, 0)
    total = jnp.zeros(lhs.shape, F32)
    for j in range(half):
        total = total + jnp.where((row == j) | (row == j + half), nt(lhs, ref[0, j]), 0.0)
    return total[:half] + total[half:]


def slope_row(ref, side, j, full):
    sign = jnp.where(side == 0, 1.0, -1.0)
    return sign * jnp.sum(ref[1 - side, j].astype(F32) * full, 0, keepdims=True)


def product_kernel(keep_ref, out_ref):
    for j in range(out_ref.shape[0]):
        out_ref[j] = nt(keep_ref[3, j], keep_ref[2, j])


def kappa_kernel(keep_ref, recv_ref, rows_ref, kappa_ref):
    half = kappa_ref.shape[0]
    kappa_ref[...] = weighted_keys(keep_ref, rows_ref[1, :half, :]) + weighted_keys(recv_ref, rows_ref[1, half:, :])


def inside_kernel(pair, keep_ref, recv_ref, rows_ref, near_ref, product_ref, attn_ref, *refs):
    if pair:
        other_ref, mine_ref, send_ref, dg_ref, scale_ref = refs
    else:
        (scale_ref,) = refs
    par, chip = place()
    _, half, width, count = keep_ref.shape
    const = 1.0 / width
    cumul = rows_ref[0]
    columns = cumul.T
    tail, head, _ = scales(cumul)
    scale_ref[0] = tail
    scale_ref[1] = head
    causal = iota((count, count), 0) >= iota((count, count), 1)
    both = (keep_ref, recv_ref)
    side = chip
    if pair:
        enters = par == 1 - side
        for j in range(half):
            line = jnp.where(
                enters, scale_ref[1 - side, j : j + 1, :], scale_ref[1 - side, half + j : half + j + 1, :]
            )
            left = jnp.where(enters, keep_ref[1 - side, j], recv_ref[1 - side, j])
            right = jnp.where(enters, keep_ref[3 - side, j], recv_ref[3 - side, j])
            other_ref[0, j] = nn((left.astype(F32) * line).astype(BF16), right)
        send_ref[0, half] = jnp.zeros((count, width), BF16)
        send_ref[0, half, : 2 * half] = hi_lo(rows_ref[1, half:, :])
    for rel, ref in enumerate(both):
        block = par if rel == 0 else 1 - par
        slopes = []
        for j in range(half):
            at = rel * half + j
            decay = jnp.exp(jnp.where(causal, columns[:, at : at + 1] - cumul[at : at + 1], -1e30))
            product = product_ref[j] if rel == 0 else nt(ref[3, j], ref[2, j])
            weight = (const * product * decay).astype(BF16)
            query = nt(ref[0, j], weight)
            key = nn(ref[1, j], weight)
            if pair:
                attn_ref[0, rel, j] = jnp.where(side == 0, key, query)
                cross = nt(near_ref[0, j], ref[3 - side, j])
                factor = jnp.where(block == side, 0.0, const) * scale_ref[1 - side, at : at + 1, :]
                full = jnp.where(side == 0, query, key) + factor * cross
                (mine_ref if rel == 0 else send_ref)[0, j] = full.astype(BF16).T
                slopes.append(slope_row(ref, side, j, full))
            else:
                attn_ref[0, rel, j] = query
                attn_ref[1, rel, j] = key
        if pair:
            dg_ref[rel] = jnp.concatenate(slopes, 0)


def outside_kernel(pair, keep_ref, recv_ref, rows_ref, state_ref, near_ref, attn_ref, kappa_ref, *refs):
    if pair:
        dg_ref, full_ref, suffix_ref, pieces_ref, scale_ref = refs
    else:
        full_ref, suffix_ref, pieces_ref, scale_ref = refs
    par, chip = place()
    _, half, width, count = keep_ref.shape
    const = 1.0 / width
    cumul = rows_ref[0]
    tail, head, ends = scales(cumul)
    scale_ref[0] = tail
    scale_ref[1] = head
    both = (keep_ref, recv_ref)
    all_slopes = []
    for rel, ref in enumerate(both):
        block = par if rel == 0 else 1 - par
        slopes = dg_ref[rel] if pair else jnp.zeros((half, count), F32)
        for at, side in enumerate((1 - chip,) if pair else (0, 1)):
            enters = block == side
            lines = []
            for j in range(half):
                come = state_ref[at, j].astype(F32)
                passed = (1 - rel) * half + j
                ratio = jnp.where(enters, 1.0, ends[passed : passed + 1])
                known = ratio * come + jnp.where(enters, 0.0, 1.0) * near_ref[at, j]
                cross = nt(known.astype(BF16), ref[3 - side, j])
                factor = const * scale_ref[1 - side, rel * half + j : rel * half + j + 1, :]
                full = attn_ref[at, rel, j] + factor * cross
                full_ref[at, rel, j] = full.astype(BF16)
                lines.append(slope_row(ref, side, j, full))
            slopes = slopes + jnp.concatenate(lines, 0)
        all_slopes.append(slopes)
    slope = jnp.concatenate(all_slopes, 0)
    suffix = exact(slope, jnp.where(iota((count, count), 0) >= iota((count, count), 1), 1.0, 0.0))
    sums = jnp.broadcast_to(suffix[:, :1], suffix.shape)
    first = jnp.where(par == 0, 1.0, 0.0)
    mine = suffix[:half] + first * sums[half:]
    other = suffix[half:] + (1.0 - first) * sums[:half]
    suffix_ref[0] = mine
    suffix_ref[1] = other
    total = sums[:half] + sums[half:]
    before = jnp.where(chip == 1, 1.0, 0.0) if pair else 1.0
    partial = (
        weighted_keys(keep_ref, mine * rows_ref[1, :half, :])
        + weighted_keys(recv_ref, other * rows_ref[1, half:, :])
        + before * (total * kappa_ref[...])
    )
    parts = lax.axis_size("dp")
    ranks = pieces_ref.shape[0] // parts
    piece, slot = width // parts, width // half
    here = iota((half, width), 1) // slot == iota((half, width), 0)
    totals = jnp.sum(jnp.where(here, total, 0.0), 0, keepdims=True)
    for i in range(parts):
        turned = partial if i == 0 else pltpu.roll(partial, width - i * piece, 1)
        turned = pltpu.roll(turned, 0, 1, stride=slot, stride_axis=0)
        line = jnp.sum(jnp.where(here, turned, 0.0), 0, keepdims=True)
        sent = jnp.concatenate([line, totals], 0)
        pieces_ref[pl.ds(i * ranks, ranks)] = jnp.broadcast_to(sent[None], (ranks, 2, width))


def turn_kernel(full_ref, suffix_ref, rows_ref, mine_ref, send_ref):
    sides, _, half, width, count = full_ref.shape
    for at in range(sides):
        for j in range(half):
            mine_ref[at, j] = full_ref[at, 0, j].T
            send_ref[at, j] = full_ref[at, 1, j].T
        send_ref[at, half] = jnp.zeros((count, width), BF16)
    if sides == 2:
        send_ref[0, half, : 2 * half] = hi_lo(rows_ref[1, half:, :])
    send_ref[sides - 1, half, : 2 * half] = hi_lo(suffix_ref[1])


def merge_kernel(pair, suffix_ref, rows_ref, *refs):
    if pair:
        mine0, recv0, mine1, recv1, query_ref, key_ref, line_ref, tmp = refs
        sources = ((mine0, recv0, 0), (mine1, recv1, 0))
    else:
        mine0, recv0, query_ref, key_ref, line_ref, tmp = refs
        sources = ((mine0, recv0, 0), (mine0, recv0, 1))
    par, chip = place()
    _, count, heads, width = query_ref.shape
    half = heads // 2
    for at, (mine, recv, side) in enumerate(sources):
        for j in range(half):
            for ref, base in ((mine, par * half), (recv, (1 - par) * half)):
                tmp[at, pl.ds(base + j, count, stride=heads), :] = ref[side, j].astype(F32)
        got = recv[side, half, : 2 * half].astype(F32)
        line_ref[at, pl.ds((1 - par) * half, half), :] = got[:half] + got[half:]
    line_ref[0, pl.ds(par * half, half), :] = rows_ref[1, :half, :]
    line_ref[1, pl.ds(par * half, half), :] = suffix_ref[0]
    first = chip if pair else 0
    query_ref[0] = tmp[first].reshape(count, heads, width).astype(BF16)
    key_ref[0] = tmp[1 - first].reshape(count, heads, width).astype(BF16)


def last_kernel(lines_ref, key_ref, gate_ref, pieces_ref, out_ref, grad_ref, buf, sems):
    _, chip = place()
    _, count, heads, width = key_ref.shape
    half = heads // 2
    parts, ranks = lax.axis_size("dp"), lax.axis_size("ctx")
    groups, slot = ranks // 2, width // half
    own = pieces_ref[pl.ds(lax.axis_index("dp") * ranks, ranks)].reshape(groups, 2, 2, width)
    beyond = sum(jnp.where(m > chip, 1.0, 0.0) * own[m, :, 1] for m in range(groups))
    lane, sub = iota((half, width), 1), iota((half, width), 0)
    chosen = [
        jnp.sum(jnp.where(lane == sub * slot, beyond[c : c + 1], 0.0), 1, keepdims=True) for c in range(2)
    ]
    after = jnp.concatenate(chosen, 0)
    slope = lines_ref[0] * (lines_ref[1] + after)
    gate = gate_ref[0]
    chunks = sems.shape[0]
    rows = count // chunks
    copies = []
    for c in range(chunks):
        for t in range(c * rows, (c + 1) * rows):
            buf[t] = (key_ref[0, t].astype(F32) + slope[:, t : t + 1] * gate).astype(BF16)
        part = pl.ds(c * rows, rows)
        copy = pltpu.make_async_copy(buf.at[part], out_ref.at[0, part], sems.at[c])
        copy.start()
        copies.append(copy)
    total = jnp.sum(pieces_ref[...].reshape(parts * groups, 2, 2, width)[:, :, 0], 0)
    fold = jnp.where(iota((width, slot), 0) % slot == iota((width, slot), 1), 1.0, 0.0)
    lines = [jnp.where(lane // slot == sub, total[c : c + 1], 0.0) for c in range(2)]
    grad_ref[...] = exact(jnp.concatenate(lines, 0), fold)[:, : width // parts]
    for copy in copies:
        copy.wait()


def across_chips(total, ends, ranks, reverse):
    step = -1 if reverse else 1

    def shift(value, chips):
        hops = [(i, i + 2 * chips * step) for i in range(ranks) if 0 <= i + 2 * chips * step < ranks]
        return lax.ppermute(value, "ctx", hops)

    value, factor = shift(total, 1), shift(ends, 1)
    reach = 1
    while 2 * reach < ranks:
        value = value + factor * shift(value, reach)
        factor = factor * shift(factor, reach)
        reach *= 2
    return value


def per_device(mesh, queries, keys, values, out_grad, gate_weight, head_bias):
    _, count, heads, width = queries.shape
    parts, ranks = mesh.shape["dp"], mesh.shape["ctx"]
    half = heads // 2
    pair = ranks == 4
    direct = parts == 8
    swap = [(i, i ^ 1) for i in range(ranks)]

    def shape(*dims, dtype=BF16):
        return jax.ShapeDtypeStruct(dims, dtype)

    bias = jnp.broadcast_to(head_bias.astype(F32)[:, None], (heads, width))

    quad = shape(4, half, width, count)
    keep, send = call(
        split_kernel,
        "split_heads",
        (quad, quad),
        (keys, queries, values, out_grad),
        [
            pltpu.VMEM((4, count, heads, width), BF16),
            pltpu.VMEM((4, 2, half, width, count), BF16),
            pltpu.SemaphoreType.DMA((4,)),
            pltpu.SemaphoreType.DMA((4, 2)),
        ],
        3.0,
        in_specs=[HBM] * 4,
        out_specs=(HBM, HBM),
        limit=60 * 1024 * 1024,
    )
    if direct:
        nearby = lax.ppermute(gate_weight, "dp", [(i, i ^ 1) for i in range(parts)])
        nearby, send = lax.optimization_barrier((nearby, send))
        two = jnp.stack([gate_weight, nearby])
        gates = [two] + [
            lax.ppermute(two, "dp", [(i, i ^ far) for i in range(parts)]) for far in range(2, parts, 2)
        ]
    else:
        gates = [lax.all_gather(gate_weight, "dp", axis=1, tiled=True)]
    recv = lax.ppermute(send, "ctx", swap)
    (products,) = call(
        product_kernel, "products", (shape(half, count, count, dtype=F32),), (keep,), (), 1.0
    )
    *gates, products = lax.optimization_barrier((*gates, products))

    sides = 1 if pair else 2
    lines = pltpu.VMEM((2, heads, count), F32)
    state = shape(sides, half, width, width, dtype=BF16 if pair else F32)
    (gate_full,) = call(
        functools.partial(weight_kernel, direct),
        "gate_weights",
        (shape(2, heads, width, dtype=F32),),
        (*gates, bias),
        (),
        10.0,
    )
    total, near, rows = call(
        functools.partial(gate_kernel, pair),
        "gate_states",
        (state, state, shape(2, heads, count, dtype=F32)),
        (gate_full, keep, recv),
        [lines],
        1.3,
    )

    attn_shape = shape(sides, 2, half, width, count, dtype=F32)
    mine_shape = shape(sides, half, count, width)
    send_shape = shape(sides, half + 1, count, width)
    slope_shape = shape(2, half, count, dtype=F32)

    def inside(*outs):
        return call(
            functools.partial(inside_kernel, pair),
            "inside_block",
            (attn_shape, *outs),
            (keep, recv, rows, near, products),
            [lines],
            4.0,
        )

    (kappa,) = call(
        kappa_kernel, "kappa", (shape(half, width, dtype=F32),), (keep, recv, rows), (), 0.3
    )
    if pair:
        opposite = [(i, i ^ 2) for i in range(ranks)]
        states = lax.ppermute(total, "ctx", opposite)
        near_shape = shape(1, half, width, width, dtype=F32)
        attn, near, mine_local, send_local, slopes = inside(near_shape, mine_shape, send_shape, slope_shape)
        kappa = lax.ppermute(kappa, "ctx", opposite)
        recv_local = lax.ppermute(send_local, "ctx", swap)
        more = (slopes,)
        local = (mine_local, recv_local)
    else:
        ends = jnp.exp(rows[0, :half, -1] + rows[0, half:, -1])[:, None, None]
        states = jnp.stack(
            [across_chips(total[0], ends, ranks, False), across_chips(total[1], ends, ranks, True)]
        )
        (attn,) = inside()
        kappa = across_chips(kappa, jnp.ones((half, 1), F32), ranks, False)
        more = ()
        local = ()
    full, suffix, pieces = call(
        functools.partial(outside_kernel, pair),
        "outside_block",
        (shape(sides, 2, half, width, count), slope_shape, shape(parts * ranks, 2, width, dtype=F32)),
        (keep, recv, rows, states, near, attn, kappa, *more),
        [lines],
        1.5,
    )
    pieces = lax.all_to_all(pieces, ("dp", "ctx"), 0, 0, tiled=True)

    mine, send = call(turn_kernel, "turn_planes", (mine_shape, send_shape), (full, suffix, rows), (), 1.0)
    recv_out = lax.ppermute(send, "ctx", swap)
    whole = shape(1, count, heads, width)
    query_grad, key_part, out_lines = call(
        functools.partial(merge_kernel, pair),
        "merge_heads",
        (whole, whole, shape(2, heads, count, dtype=F32)),
        (suffix, rows, *local, mine, recv_out),
        [pltpu.VMEM((2, count * heads, width), F32)],
        2.0,
    )
    key_grad, gate_grad = call(
        last_kernel,
        "key_gradient",
        (whole, shape(heads, width // parts, dtype=F32)),
        (out_lines, key_part, gate_full, pieces),
        [pltpu.VMEM((count, heads, width), BF16), pltpu.SemaphoreType.DMA((4,))],
        1.0,
        out_specs=(ANY, VMEM),
    )
    return query_grad, key_grad, gate_grad


def solution(mesh):
    return jax.shard_map(
        functools.partial(per_device, mesh),
        mesh=mesh,
        in_specs=(
            P("dp", "ctx", None, None),
            P("dp", "ctx", None, None),
            P("dp", "ctx", None, None),
            P("dp", "ctx", None, None),
            P(None, "dp"),
            P(),
        ),
        out_specs=(P("dp", "ctx", None, None), P("dp", "ctx", None, None), P(None, "dp")),
        check_vma=False,
    )
```

```python
import functools

import jax
import jax.numpy as jnp
from jax import lax
from jax.experimental import pallas as pl
from jax.experimental.pallas import tpu as pltpu
from jax.sharding import PartitionSpec as P

F32 = jnp.float32
BF16 = jnp.bfloat16
VMEM = pl.BlockSpec(memory_space=pltpu.VMEM)
ANY = pl.BlockSpec(memory_space=pl.ANY)
HBM = pl.BlockSpec(memory_space=pltpu.HBM)
LIMIT = 24 * 1024 * 1024


def nn(a, b):
    return lax.dot_general(a, b, (((1,), (0,)), ((), ())), preferred_element_type=F32)


def nt(a, b):
    return lax.dot_general(a, b, (((1,), (1,)), ((), ())), preferred_element_type=F32)


def exact(a, b):
    return lax.dot_general(
        a, b, (((1,), (0,)), ((), ())), precision=lax.Precision.HIGHEST, preferred_element_type=F32
    )


def iota(shape, dim):
    return lax.broadcasted_iota(jnp.int32, shape, dim)


def place():
    mine = lax.axis_index("ctx")
    return lax.rem(mine, 2), lax.div(mine, 2)


def hi_lo(rows):
    hi = rows.astype(BF16)
    return jnp.concatenate([hi, (rows - hi.astype(F32)).astype(BF16)], 0)


def call(kernel, name, out_shape, operands, scratch=(), micros=1.0, in_specs=None, out_specs=None, limit=LIMIT):
    outs = len(out_shape)
    return pl.pallas_call(
        kernel,
        out_shape=out_shape,
        in_specs=in_specs or [VMEM] * len(operands),
        out_specs=out_specs or (VMEM,) * outs,
        scratch_shapes=list(scratch),
        compiler_params=pltpu.CompilerParams(vmem_limit_bytes=limit),
        cost_estimate=pl.CostEstimate(
            flops=0, bytes_accessed=int(micros * 3_000_000), transcendentals=0
        ),
        name=name,
    )(*operands)


def split_kernel(k_ref, q_ref, v_ref, g_ref, gate_ref, keep_ref, send_ref, copy_ref, buf, sems):
    par, _ = place()
    half = keep_ref.shape[1]
    loads = [
        pltpu.make_async_copy(ref.at[0], buf.at[at], sems.at[at])
        for at, ref in enumerate((k_ref, q_ref, v_ref, g_ref))
    ]
    for load in loads:
        load.start()
    gate = pltpu.make_async_copy(gate_ref, copy_ref, sems.at[len(loads)])
    gate.start()
    for at, load in enumerate(loads):
        load.wait()
        planes = jnp.swapaxes(buf[at], 0, 1)
        for j in range(half):
            first, second = planes[j], planes[half + j]
            if at < 2:
                first, second = first.T, second.T
            keep_ref[at, j] = jnp.where(par == 0, first, second)
            send_ref[at, j] = jnp.where(par == 0, second, first)
    gate.wait()


def scales(rows):
    end = jnp.broadcast_to(rows[:, -1:], rows.shape)
    return jnp.exp(end - rows), jnp.exp(rows), jnp.exp(end)


def weight_kernel(direct, *refs):
    *gates, bias_ref, gate_ref = refs
    heads, width = gate_ref.shape[1:]
    if direct:
        index = lax.axis_index("dp")
        full = jnp.zeros((heads, width), F32)
        for r, ref in enumerate(gates):
            for low in range(2):
                piece = ref.shape[2]
                owner = jnp.bitwise_xor(index, 2 * r + low)
                pick = iota((piece, width), 1) == iota((piece, width), 0) + owner * piece
                full = full + nn(ref[low], jnp.where(pick, 1.0, 0.0).astype(BF16))
    else:
        full = gates[0][...].astype(F32)
    gate_ref[0] = full
    gate_ref[1] = bias_ref[...]


def gate_kernel(pair, gate_ref, keep_ref, recv_ref, total_ref, near_ref, rows_ref, scale_ref):
    par, chip = place()
    _, half, width, count = keep_ref.shape
    weights = gate_ref[0, pl.ds(par * half, half), :].astype(BF16)
    bias = gate_ref[1, pl.ds(par * half, half), :]
    row = iota((half, count), 0)
    logits = []
    for ref in (keep_ref, recv_ref):
        logit = bias
        for j in range(half):
            logit = logit + jnp.where(row == j, nn(weights, ref[0, j]), 0.0)
        logits.append(logit)
    logit = jnp.concatenate(logits, 0)
    decay = -(jnp.maximum(logit, 0.0) + jnp.log1p(jnp.exp(-jnp.abs(logit))))
    cumul = exact(decay, jnp.where(iota((count, count), 0) <= iota((count, count), 1), 1.0, 0.0))
    rows_ref[0] = cumul
    rows_ref[1] = -1.0 / (1.0 + jnp.exp(-logit))
    tail, head, ends = scales(cumul)
    scale_ref[0] = tail
    scale_ref[1] = head
    for at, side in enumerate((chip,) if pair else (0, 1)):
        enters = par == side
        for j in range(half):
            states = []
            for rel, ref in enumerate((keep_ref, recv_ref)):
                line = scale_ref[side, rel * half + j : rel * half + j + 1, :]
                scaled = (ref[side, j].astype(F32) * line).astype(BF16)
                states.append(nn(scaled, ref[2 + side, j]))
            own, other = states
            passed = (
                jnp.where(enters, ends[half + j : half + j + 1], 1.0) * own
                + jnp.where(enters, 1.0, ends[j : j + 1]) * other
            )
            total_ref[at, j] = passed.astype(total_ref.dtype)
            near_ref[at, j] = jnp.where(enters, own, other).astype(near_ref.dtype)


def weighted_keys(ref, rows):
    half = rows.shape[0]
    lhs = hi_lo(rows)
    row = iota(lhs.shape, 0)
    total = jnp.zeros(lhs.shape, F32)
    for j in range(half):
        total = total + jnp.where((row == j) | (row == j + half), nt(lhs, ref[0, j]), 0.0)
    return total[:half] + total[half:]


def slope_row(ref, side, j, full):
    sign = jnp.where(side == 0, 1.0, -1.0)
    return sign * jnp.sum(ref[1 - side, j].astype(F32) * full, 0, keepdims=True)


def product_kernel(keep_ref, out_ref):
    for j in range(out_ref.shape[0]):
        out_ref[j] = nt(keep_ref[3, j], keep_ref[2, j])


def kappa_kernel(keep_ref, recv_ref, rows_ref, kappa_ref):
    half = kappa_ref.shape[0]
    kappa_ref[...] = weighted_keys(keep_ref, rows_ref[1, :half, :]) + weighted_keys(recv_ref, rows_ref[1, half:, :])


def inside_kernel(pair, keep_ref, recv_ref, rows_ref, near_ref, product_ref, attn_ref, *refs):
    if pair:
        other_ref, mine_ref, send_ref, dg_ref, scale_ref = refs
    else:
        (scale_ref,) = refs
    par, chip = place()
    _, half, width, count = keep_ref.shape
    const = 1.0 / width
    cumul = rows_ref[0]
    columns = cumul.T
    tail, head, _ = scales(cumul)
    scale_ref[0] = tail
    scale_ref[1] = head
    causal = iota((count, count), 0) >= iota((count, count), 1)
    both = (keep_ref, recv_ref)
    side = chip
    if pair:
        enters = par == 1 - side
        for j in range(half):
            line = jnp.where(
                enters, scale_ref[1 - side, j : j + 1, :], scale_ref[1 - side, half + j : half + j + 1, :]
            )
            left = jnp.where(enters, keep_ref[1 - side, j], recv_ref[1 - side, j])
            right = jnp.where(enters, keep_ref[3 - side, j], recv_ref[3 - side, j])
            other_ref[0, j] = nn((left.astype(F32) * line).astype(BF16), right)
        send_ref[0, half] = jnp.zeros((count, width), BF16)
        send_ref[0, half, : 2 * half] = hi_lo(rows_ref[1, half:, :])
    for rel, ref in enumerate(both):
        block = par if rel == 0 else 1 - par
        slopes = []
        for j in range(half):
            at = rel * half + j
            decay = jnp.exp(jnp.where(causal, columns[:, at : at + 1] - cumul[at : at + 1], -1e30))
            product = product_ref[j] if rel == 0 else nt(ref[3, j], ref[2, j])
            weight = (const * product * decay).astype(BF16)
            query = nt(ref[0, j], weight)
            key = nn(ref[1, j], weight)
            if pair:
                attn_ref[0, rel, j] = jnp.where(side == 0, key, query)
                cross = nt(near_ref[0, j], ref[3 - side, j])
                factor = jnp.where(block == side, 0.0, const) * scale_ref[1 - side, at : at + 1, :]
                full = jnp.where(side == 0, query, key) + factor * cross
                (mine_ref if rel == 0 else send_ref)[0, j] = full.astype(BF16)
                slopes.append(slope_row(ref, side, j, full))
            else:
                attn_ref[0, rel, j] = query
                attn_ref[1, rel, j] = key
        if pair:
            dg_ref[rel] = jnp.concatenate(slopes, 0)


def outside_kernel(pair, keep_ref, recv_ref, rows_ref, state_ref, near_ref, attn_ref, kappa_ref, *refs):
    if pair:
        dg_ref, mine_ref, send_ref, suffix_ref, pieces_ref, scale_ref = refs
    else:
        mine_ref, send_ref, suffix_ref, pieces_ref, scale_ref = refs
    par, chip = place()
    _, half, width, count = keep_ref.shape
    const = 1.0 / width
    cumul = rows_ref[0]
    tail, head, ends = scales(cumul)
    scale_ref[0] = tail
    scale_ref[1] = head
    both = (keep_ref, recv_ref)
    all_slopes = []
    for rel, ref in enumerate(both):
        block = par if rel == 0 else 1 - par
        slopes = dg_ref[rel] if pair else jnp.zeros((half, count), F32)
        for at, side in enumerate((1 - chip,) if pair else (0, 1)):
            enters = block == side
            lines = []
            for j in range(half):
                come = state_ref[at, j].astype(F32)
                passed = (1 - rel) * half + j
                ratio = jnp.where(enters, 1.0, ends[passed : passed + 1])
                known = ratio * come + jnp.where(enters, 0.0, 1.0) * near_ref[at, j]
                cross = nt(known.astype(BF16), ref[3 - side, j])
                factor = const * scale_ref[1 - side, rel * half + j : rel * half + j + 1, :]
                full = attn_ref[at, rel, j] + factor * cross
                (mine_ref if rel == 0 else send_ref)[at, j] = full.astype(BF16)
                lines.append(slope_row(ref, side, j, full))
            slopes = slopes + jnp.concatenate(lines, 0)
        all_slopes.append(slopes)
    slope = jnp.concatenate(all_slopes, 0)
    suffix = exact(slope, jnp.where(iota((count, count), 0) >= iota((count, count), 1), 1.0, 0.0))
    sums = jnp.broadcast_to(suffix[:, :1], suffix.shape)
    first = jnp.where(par == 0, 1.0, 0.0)
    mine = suffix[:half] + first * sums[half:]
    other = suffix[half:] + (1.0 - first) * sums[:half]
    suffix_ref[...] = mine
    sides = send_ref.shape[0]
    for at in range(sides):
        send_ref[at, half] = jnp.zeros((width, count), BF16)
    if sides == 2:
        send_ref[0, half, : 2 * half] = hi_lo(rows_ref[1, half:, :])
    send_ref[sides - 1, half, : 2 * half] = hi_lo(other)
    total = sums[:half] + sums[half:]
    before = jnp.where(chip == 1, 1.0, 0.0) if pair else 1.0
    partial = (
        weighted_keys(keep_ref, mine * rows_ref[1, :half, :])
        + weighted_keys(recv_ref, other * rows_ref[1, half:, :])
        + before * (total * kappa_ref[...])
    )
    parts = lax.axis_size("dp")
    ranks = pieces_ref.shape[0] // parts
    piece, slot = width // parts, width // half
    here = iota((half, width), 1) // slot == iota((half, width), 0)
    totals = jnp.sum(jnp.where(here, total, 0.0), 0, keepdims=True)
    for i in range(parts):
        turned = partial if i == 0 else pltpu.roll(partial, width - i * piece, 1)
        turned = pltpu.roll(turned, 0, 1, stride=slot, stride_axis=0)
        line = jnp.sum(jnp.where(here, turned, 0.0), 0, keepdims=True)
        sent = jnp.concatenate([line, totals], 0)
        pieces_ref[pl.ds(i * ranks, ranks)] = jnp.broadcast_to(sent[None], (ranks, 2, width))


def merge_kernel(pair, suffix_ref, rows_ref, *refs):
    if pair:
        mine0, recv0, mine1, recv1, query_ref, key_ref, line_ref, tmp = refs
        sources = ((mine0, recv0, 0), (mine1, recv1, 0))
    else:
        mine0, recv0, query_ref, key_ref, line_ref, tmp = refs
        sources = ((mine0, recv0, 0), (mine0, recv0, 1))
    par, chip = place()
    _, count, heads, width = query_ref.shape
    half = heads // 2
    for at, (mine, recv, side) in enumerate(sources):
        for j in range(half):
            for ref, base in ((mine, par * half), (recv, (1 - par) * half)):
                tmp[at, pl.ds(base + j, count, stride=heads), :] = ref[side, j].T.astype(F32)
        got = recv[side, half, : 2 * half].astype(F32)
        line_ref[at, pl.ds((1 - par) * half, half), :] = got[:half] + got[half:]
    line_ref[0, pl.ds(par * half, half), :] = rows_ref[1, :half, :]
    line_ref[1, pl.ds(par * half, half), :] = suffix_ref[...]
    first = chip if pair else 0
    query_ref[0] = tmp[first].reshape(count, heads, width).astype(BF16)
    key_ref[0] = tmp[1 - first].reshape(count, heads, width).astype(BF16)


def last_kernel(lines_ref, key_ref, gate_ref, pieces_ref, out_ref, grad_ref, buf, small, sems):
    _, chip = place()
    _, count, heads, width = key_ref.shape
    half = heads // 2
    parts, ranks = lax.axis_size("dp"), lax.axis_size("ctx")
    groups, slot = ranks // 2, width // half
    own = pieces_ref[pl.ds(lax.axis_index("dp") * ranks, ranks)].reshape(groups, 2, 2, width)
    beyond = sum(jnp.where(m > chip, 1.0, 0.0) * own[m, :, 1] for m in range(groups))
    lane, sub = iota((half, width), 1), iota((half, width), 0)
    chosen = [
        jnp.sum(jnp.where(lane == sub * slot, beyond[c : c + 1], 0.0), 1, keepdims=True) for c in range(2)
    ]
    after = jnp.concatenate(chosen, 0)
    slope = lines_ref[0] * (lines_ref[1] + after)
    gate = gate_ref[0]
    for t in range(count):
        buf[t] = (key_ref[0, t].astype(F32) + slope[:, t : t + 1] * gate).astype(BF16)
    key_copy = pltpu.make_async_copy(buf, out_ref.at[0], sems.at[0])
    key_copy.start()
    total = jnp.sum(pieces_ref[...].reshape(parts * groups, 2, 2, width)[:, :, 0], 0)
    fold = jnp.where(iota((width, slot), 0) % slot == iota((width, slot), 1), 1.0, 0.0)
    lines = [jnp.where(lane // slot == sub, total[c : c + 1], 0.0) for c in range(2)]
    small[...] = exact(jnp.concatenate(lines, 0), fold)[:, : width // parts]
    grad_copy = pltpu.make_async_copy(small, grad_ref, sems.at[1])
    grad_copy.start()
    key_copy.wait()
    grad_copy.wait()


def across_chips(total, ends, ranks, reverse):
    step = -1 if reverse else 1

    def shift(value, chips):
        hops = [(i, i + 2 * chips * step) for i in range(ranks) if 0 <= i + 2 * chips * step < ranks]
        return lax.ppermute(value, "ctx", hops)

    value, factor = shift(total, 1), shift(ends, 1)
    reach = 1
    while 2 * reach < ranks:
        value = value + factor * shift(value, reach)
        factor = factor * shift(factor, reach)
        reach *= 2
    return value


def per_device(mesh, queries, keys, values, out_grad, gate_weight, head_bias):
    _, count, heads, width = queries.shape
    parts, ranks = mesh.shape["dp"], mesh.shape["ctx"]
    half = heads // 2
    pair = ranks == 4
    direct = parts == 8
    swap = [(i, i ^ 1) for i in range(ranks)]

    def shape(*dims, dtype=BF16):
        return jax.ShapeDtypeStruct(dims, dtype)

    bias = jnp.broadcast_to(head_bias.astype(F32)[:, None], (heads, width))

    quad = shape(4, half, width, count)
    pinned = [
        pltpu.with_memory_space_constraint(x, pltpu.HBM)
        for x in (keys, queries, values, out_grad, gate_weight)
    ]
    keep, send, gate_copy = call(
        split_kernel,
        "split_heads",
        (quad, quad, shape(*gate_weight.shape)),
        pinned,
        [pltpu.VMEM((4, count, heads, width), BF16), pltpu.SemaphoreType.DMA((5,))],
        3.0,
        in_specs=[HBM] * 5,
    )
    if direct:
        nearby = lax.ppermute(gate_weight, "dp", [(i, i ^ 1) for i in range(parts)])
        nearby, send = lax.optimization_barrier((nearby, send))
        two = jnp.stack([gate_copy, nearby])
        gates = [
            lax.ppermute(two, "dp", [(i, i ^ far) for i in range(parts)])
            for far in (4, 6, 2)
        ]
    else:
        gates = [lax.all_gather(gate_weight, "dp", axis=1, tiled=True)]
    recv = lax.ppermute(send, "ctx", swap)
    (products,) = call(
        product_kernel, "products", (shape(half, count, count, dtype=F32),), (keep,), (), 1.0
    )
    *gates, products = lax.optimization_barrier((*gates, products))
    if direct:
        gates = [two, gates[2], gates[0], gates[1]]

    sides = 1 if pair else 2
    lines = pltpu.VMEM((2, heads, count), F32)
    state = shape(sides, half, width, width, dtype=BF16 if pair else F32)
    (gate_full,) = call(
        functools.partial(weight_kernel, direct),
        "gate_weights",
        (shape(2, heads, width, dtype=F32),),
        (*gates, bias),
        (),
        10.0,
    )
    total, near, rows = call(
        functools.partial(gate_kernel, pair),
        "gate_states",
        (state, state, shape(2, heads, count, dtype=F32)),
        (gate_full, keep, recv),
        [lines],
        1.3,
    )

    attn_shape = shape(sides, 2, half, width, count, dtype=F32)
    mine_shape = shape(sides, half, width, count)
    send_shape = shape(sides, half + 1, width, count)
    slope_shape = shape(2, half, count, dtype=F32)

    def inside(*outs):
        return call(
            functools.partial(inside_kernel, pair),
            "inside_block",
            (attn_shape, *outs),
            (keep, recv, rows, near, products),
            [lines],
            4.0,
        )

    (kappa,) = call(
        kappa_kernel, "kappa", (shape(half, width, dtype=F32),), (keep, recv, rows), (), 0.3
    )
    if pair:
        opposite = [(i, i ^ 2) for i in range(ranks)]
        states = lax.ppermute(total, "ctx", opposite)
        near_shape = shape(1, half, width, width, dtype=F32)
        attn, near, mine_local, send_local, slopes = inside(near_shape, mine_shape, send_shape, slope_shape)
        kappa = lax.ppermute(kappa, "ctx", opposite)
        recv_local = lax.ppermute(send_local, "ctx", swap)
        more = (slopes,)
        local = (mine_local, recv_local)
    else:
        ends = jnp.exp(rows[0, :half, -1] + rows[0, half:, -1])[:, None, None]
        states = jnp.stack(
            [across_chips(total[0], ends, ranks, False), across_chips(total[1], ends, ranks, True)]
        )
        (attn,) = inside()
        kappa = across_chips(kappa, jnp.ones((half, 1), F32), ranks, False)
        more = ()
        local = ()
    mine, send, suffix, pieces = call(
        functools.partial(outside_kernel, pair),
        "outside_block",
        (mine_shape, send_shape, shape(half, count, dtype=F32), shape(parts * ranks, 2, width, dtype=F32)),
        (keep, recv, rows, states, near, attn, kappa, *more),
        [lines],
        1.5,
    )
    pieces = lax.all_to_all(pieces, ("dp", "ctx"), 0, 0, tiled=True)
    recv_out = lax.ppermute(send, "ctx", swap)
    whole = shape(1, count, heads, width)
    query_grad, key_part, out_lines = call(
        functools.partial(merge_kernel, pair),
        "merge_heads",
        (whole, whole, shape(2, heads, count, dtype=F32)),
        (suffix, rows, *local, mine, recv_out),
        [pltpu.VMEM((2, count * heads, width), F32)],
        2.0,
    )
    key_grad, gate_grad = call(
        last_kernel,
        "key_gradient",
        (whole, shape(heads, width // parts, dtype=F32)),
        (out_lines, key_part, gate_full, pieces),
        [
            pltpu.VMEM((count, heads, width), BF16),
            pltpu.VMEM((heads, width // parts), F32),
            pltpu.SemaphoreType.DMA((2,)),
        ],
        1.0,
        out_specs=(ANY, ANY),
    )
    return query_grad, key_grad, gate_grad


def solution(mesh):
    return jax.shard_map(
        functools.partial(per_device, mesh),
        mesh=mesh,
        in_specs=(
            P("dp", "ctx", None, None),
            P("dp", "ctx", None, None),
            P("dp", "ctx", None, None),
            P("dp", "ctx", None, None),
            P(None, "dp"),
            P(),
        ),
        out_specs=(P("dp", "ctx", None, None), P("dp", "ctx", None, None), P(None, "dp")),
        check_vma=False,
    )
```

```python
import functools

import jax
import jax.numpy as jnp
from jax import lax
from jax.experimental import pallas as pl
from jax.experimental.pallas import tpu as pltpu
from jax.sharding import PartitionSpec as P

F32 = jnp.float32
BF16 = jnp.bfloat16
VMEM = pl.BlockSpec(memory_space=pltpu.VMEM)
ANY = pl.BlockSpec(memory_space=pl.ANY)
HBM = pl.BlockSpec(memory_space=pltpu.HBM)
LIMIT = 24 * 1024 * 1024


def nn(a, b):
    return lax.dot_general(a, b, (((1,), (0,)), ((), ())), preferred_element_type=F32)


def nt(a, b):
    return lax.dot_general(a, b, (((1,), (1,)), ((), ())), preferred_element_type=F32)


def exact(rows, mask):
    count = rows.shape[0]
    parts, rest = [], rows
    for _ in range(3):
        part = rest.astype(BF16)
        parts.append(part)
        rest = rest - part.astype(F32)
    out = nn(jnp.concatenate(parts, 0), jnp.where(mask, 1.0, 0.0).astype(BF16))
    return out[:count] + (out[count : 2 * count] + out[2 * count :])


def iota(shape, dim):
    return lax.broadcasted_iota(jnp.int32, shape, dim)


def place():
    mine = lax.axis_index("ctx")
    return lax.rem(mine, 2), lax.div(mine, 2)


def hi_lo(rows):
    hi = rows.astype(BF16)
    return jnp.concatenate([hi, (rows - hi.astype(F32)).astype(BF16)], 0)


def call(kernel, name, out_shape, operands, scratch=(), micros=1.0, in_specs=None, out_specs=None, limit=LIMIT):
    outs = len(out_shape)
    return pl.pallas_call(
        kernel,
        out_shape=out_shape,
        in_specs=in_specs or [VMEM] * len(operands),
        out_specs=out_specs or (VMEM,) * outs,
        scratch_shapes=list(scratch),
        compiler_params=pltpu.CompilerParams(vmem_limit_bytes=limit),
        cost_estimate=pl.CostEstimate(
            flops=0, bytes_accessed=int(micros * 3_000_000), transcendentals=0
        ),
        name=name,
    )(*operands)


def split_kernel(k_ref, q_ref, v_ref, g_ref, gate_ref, keep_ref, send_ref, copy_ref, buf, sems):
    par, _ = place()
    half = keep_ref.shape[1]
    loads = [
        pltpu.make_async_copy(ref.at[0], buf.at[at], sems.at[at])
        for at, ref in enumerate((k_ref, q_ref, v_ref, g_ref))
    ]
    for load in loads:
        load.start()
    gate = pltpu.make_async_copy(gate_ref, copy_ref, sems.at[len(loads)])
    gate.start()
    for at, load in enumerate(loads):
        load.wait()
        planes = jnp.swapaxes(buf[at], 0, 1)
        for j in range(half):
            first, second = planes[j], planes[half + j]
            if at < 2:
                first, second = first.T, second.T
            keep_ref[at, j] = jnp.where(par == 0, first, second)
            send_ref[at, j] = jnp.where(par == 0, second, first)
    gate.wait()


def scales(rows):
    end = jnp.broadcast_to(rows[:, -1:], rows.shape)
    return jnp.exp(end - rows), jnp.exp(rows), jnp.exp(end)


def whole_gate(direct, gates):
    index = lax.axis_index("dp")
    if not direct:
        return gates[0][...].astype(F32)
    heads, piece = gates[0].shape[1:]
    width = piece * lax.axis_size("dp")
    full = jnp.zeros((heads, width), F32)
    for r, ref in enumerate(gates):
        for low in range(2):
            owner = jnp.bitwise_xor(index, 2 * r + low)
            pick = iota((piece, width), 1) == iota((piece, width), 0) + owner * piece
            full = full + nn(ref[low], jnp.where(pick, 1.0, 0.0).astype(BF16))
    return full


def gate_kernel(direct, pair, *refs):
    *gates, bias_ref, keep_ref, recv_ref, total_ref, near_ref, rows_ref, gate_ref, scale_ref = refs
    par, chip = place()
    _, half, width, count = keep_ref.shape
    gate_ref[0] = whole_gate(direct, gates)
    same = iota((2 * half, 2 * half), 0) == iota((2 * half, 2 * half), 1)
    spread = jnp.where(same, bias_ref[...].astype(F32), 0.0).astype(BF16)
    gate_ref[1] = nn(spread, jnp.ones((2 * half, width), BF16))
    weights = gate_ref[0, pl.ds(par * half, half), :]
    bias = gate_ref[1, pl.ds(par * half, half), :]
    row, side_of = iota((half, 2 * width), 0), iota((half, 2 * width), 1) // width
    twice = jnp.concatenate([weights, weights], 1)
    logit = jnp.zeros((half, 2 * count), F32)
    for j in range(0, half, 2):
        planes = [ref[0, j : j + 2].reshape(2 * width, count) for ref in (keep_ref, recv_ref)]
        logit = logit + nn(jnp.where(row == j + side_of, twice, 0.0).astype(BF16), jnp.concatenate(planes, 1))
    logit = jnp.concatenate([bias + logit[:, :count], bias + logit[:, count:]], 0)
    decay = -(jnp.maximum(logit, 0.0) + jnp.log1p(jnp.exp(-jnp.abs(logit))))
    cumul = exact(decay, iota((count, count), 0) <= iota((count, count), 1))
    rows_ref[0] = cumul
    rows_ref[1] = -1.0 / (1.0 + jnp.exp(-logit))
    tail, head, ends = scales(cumul)
    scale_ref[0] = tail
    scale_ref[1] = head
    for at, side in enumerate((chip,) if pair else (0, 1)):
        enters = par == side
        for j in range(half):
            states = []
            for rel, ref in enumerate((keep_ref, recv_ref)):
                line = scale_ref[side, rel * half + j : rel * half + j + 1, :]
                scaled = (ref[side, j].astype(F32) * line).astype(BF16)
                states.append(nn(scaled, ref[2 + side, j]))
            own, other = states
            passed = (
                jnp.where(enters, ends[half + j : half + j + 1], 1.0) * own
                + jnp.where(enters, 1.0, ends[j : j + 1]) * other
            )
            total_ref[at, j] = passed.astype(total_ref.dtype)
            near_ref[at, j] = jnp.where(enters, own, other).astype(near_ref.dtype)


def weighted_keys(keep_ref, recv_ref, own, other):
    half, count = own.shape
    width = keep_ref.shape[2]
    lhs = jnp.concatenate([hi_lo(own), hi_lo(other)], 1)
    row = iota((2 * half, width), 0) % half
    total = jnp.zeros((2 * half, width), F32)
    for j in range(0, half, 2):
        planes = [ref[0, j : j + 2].reshape(2 * width, count) for ref in (keep_ref, recv_ref)]
        got = nt(lhs, jnp.concatenate(planes, 1))
        total = total + jnp.where(row == j, got[:, :width], 0.0) + jnp.where(row == j + 1, got[:, width:], 0.0)
    return total[:half] + total[half:]


def slope_row(ref, side, j, full):
    sign = jnp.where(side == 0, 1.0, -1.0)
    return sign * jnp.sum(ref[1 - side, j].astype(F32) * full, 0, keepdims=True)


def product_kernel(keep_ref, out_ref):
    for j in range(out_ref.shape[0]):
        out_ref[j] = nt(keep_ref[3, j], keep_ref[2, j])


def kappa_kernel(keep_ref, recv_ref, rows_ref, kappa_ref):
    half = kappa_ref.shape[0]
    kappa_ref[...] = weighted_keys(keep_ref, recv_ref, rows_ref[1, :half, :], rows_ref[1, half:, :])


def inside_kernel(pair, keep_ref, recv_ref, rows_ref, near_ref, product_ref, attn_ref, *refs):
    if pair:
        other_ref, mine_ref, send_ref, dg_ref, scale_ref = refs
    else:
        (scale_ref,) = refs
    par, chip = place()
    _, half, width, count = keep_ref.shape
    const = 1.0 / width
    cumul = rows_ref[0]
    columns = cumul.T
    tail, head, _ = scales(cumul)
    scale_ref[0] = tail
    scale_ref[1] = head
    causal = iota((count, count), 0) >= iota((count, count), 1)
    both = (keep_ref, recv_ref)
    side = chip
    if pair:
        enters = par == 1 - side
        for j in range(half):
            line = jnp.where(
                enters, scale_ref[1 - side, j : j + 1, :], scale_ref[1 - side, half + j : half + j + 1, :]
            )
            left = jnp.where(enters, keep_ref[1 - side, j], recv_ref[1 - side, j])
            right = jnp.where(enters, keep_ref[3 - side, j], recv_ref[3 - side, j])
            other_ref[0, j] = nn((left.astype(F32) * line).astype(BF16), right)
        send_ref[0, half] = jnp.zeros((count, width), BF16)
        send_ref[0, half, : 2 * half] = hi_lo(rows_ref[1, half:, :])
    for rel, ref in enumerate(both):
        block = par if rel == 0 else 1 - par
        slopes = []
        for j in range(half):
            at = rel * half + j
            decay = jnp.exp(jnp.where(causal, columns[:, at : at + 1] - cumul[at : at + 1], -1e30))
            product = product_ref[j] if rel == 0 else nt(ref[3, j], ref[2, j])
            weight = (const * product * decay).astype(BF16)
            query = nt(ref[0, j], weight)
            key = nn(ref[1, j], weight)
            if pair:
                attn_ref[0, rel, j] = jnp.where(side == 0, key, query)
                cross = nt(near_ref[0, j], ref[3 - side, j])
                factor = jnp.where(block == side, 0.0, const) * scale_ref[1 - side, at : at + 1, :]
                full = jnp.where(side == 0, query, key) + factor * cross
                (mine_ref if rel == 0 else send_ref)[0, j] = full.astype(BF16)
                slopes.append(slope_row(ref, side, j, full))
            else:
                attn_ref[0, rel, j] = query
                attn_ref[1, rel, j] = key
        if pair:
            dg_ref[rel] = jnp.concatenate(slopes, 0)


def outside_kernel(pair, keep_ref, recv_ref, rows_ref, state_ref, near_ref, attn_ref, kappa_ref, *refs):
    if pair:
        dg_ref, mine_ref, send_ref, suffix_ref, pieces_ref, scale_ref = refs
    else:
        mine_ref, send_ref, suffix_ref, pieces_ref, scale_ref = refs
    par, chip = place()
    _, half, width, count = keep_ref.shape
    const = 1.0 / width
    cumul = rows_ref[0]
    tail, head, ends = scales(cumul)
    scale_ref[0] = tail
    scale_ref[1] = head
    both = (keep_ref, recv_ref)
    all_slopes = []
    for rel, ref in enumerate(both):
        block = par if rel == 0 else 1 - par
        slopes = dg_ref[rel] if pair else jnp.zeros((half, count), F32)
        for at, side in enumerate((1 - chip,) if pair else (0, 1)):
            enters = block == side
            lines = []
            for j in range(half):
                passed = (1 - rel) * half + j
                moved = ends[passed : passed + 1] * state_ref[at, j].astype(F32) + near_ref[at, j]
                known = jnp.where(enters, state_ref[at, j].astype(F32), moved)
                cross = nt(known.astype(BF16), ref[3 - side, j])
                factor = const * scale_ref[1 - side, rel * half + j : rel * half + j + 1, :]
                full = attn_ref[at, rel, j] + factor * cross
                (mine_ref if rel == 0 else send_ref)[at, j] = full.astype(BF16)
                lines.append(slope_row(ref, side, j, full))
            slopes = slopes + jnp.concatenate(lines, 0)
        all_slopes.append(slopes)
    slope = jnp.concatenate(all_slopes, 0)
    suffix = exact(slope, iota((count, count), 0) >= iota((count, count), 1))
    sums = jnp.broadcast_to(suffix[:, :1], suffix.shape)
    first = jnp.where(par == 0, 1.0, 0.0)
    mine = suffix[:half] + first * sums[half:]
    other = suffix[half:] + (1.0 - first) * sums[:half]
    suffix_ref[...] = mine
    sides = send_ref.shape[0]
    for at in range(sides):
        send_ref[at, half] = jnp.zeros((width, count), BF16)
    if sides == 2:
        send_ref[0, half, : 2 * half] = hi_lo(rows_ref[1, half:, :])
    send_ref[sides - 1, half, : 2 * half] = hi_lo(other)
    total = sums[:half] + sums[half:]
    before = jnp.where(chip == 1, 1.0, 0.0) if pair else 1.0
    partial = (
        weighted_keys(keep_ref, recv_ref, mine * rows_ref[1, :half, :], other * rows_ref[1, half:, :])
        + before * (total * kappa_ref[...])
    )
    parts = lax.axis_size("dp")
    ranks = pieces_ref.shape[0] // parts
    piece, slot = width // parts, width // half
    here = iota((half, width), 1) // slot == iota((half, width), 0)
    totals = jnp.sum(jnp.where(here, total, 0.0), 0, keepdims=True)
    for i in range(parts):
        turned = partial if i == 0 else pltpu.roll(partial, width - i * piece, 1)
        turned = pltpu.roll(turned, 0, 1, stride=slot, stride_axis=0)
        line = jnp.sum(jnp.where(here, turned, 0.0), 0, keepdims=True)
        sent = jnp.concatenate([line, totals], 0)
        pieces_ref[pl.ds(i * ranks, ranks)] = jnp.broadcast_to(sent[None], (ranks, 2, width))


def merge_kernel(pair, gate_ref, suffix_ref, rows_ref, *refs):
    if pair:
        mine0, recv0, mine1, recv1, query_ref, base_ref, rise_ref, line_ref, tmp = refs
        sources = ((mine0, recv0, 0), (mine1, recv1, 0))
    else:
        mine0, recv0, query_ref, base_ref, rise_ref, line_ref, tmp = refs
        sources = ((mine0, recv0, 0), (mine0, recv0, 1))
    par, chip = place()
    _, count, heads, width = query_ref.shape
    half = heads // 2
    for at, (mine, recv, side) in enumerate(sources):
        for j in range(half):
            for ref, base in ((mine, par * half), (recv, (1 - par) * half)):
                tmp[at, pl.ds(base + j, count, stride=heads), :] = ref[side, j].T.astype(F32)
        got = recv[side, half, : 2 * half].astype(F32)
        line_ref[at, pl.ds((1 - par) * half, half), :] = got[:half] + got[half:]
    line_ref[0, pl.ds(par * half, half), :] = rows_ref[1, :half, :]
    line_ref[1, pl.ds(par * half, half), :] = suffix_ref[...]
    first = chip if pair else 0
    query_ref[0] = tmp[first].reshape(count, heads, width).astype(BF16)
    rise = line_ref[0]
    slope = rise * line_ref[1]
    gate = gate_ref[0]
    for t in range(count):
        known = tmp[1 - first, t * heads : (t + 1) * heads, :]
        base_ref[t] = known + slope[:, t : t + 1] * gate
        rise_ref[t] = rise[:, t : t + 1] * gate


def last_kernel(base_ref, rise_ref, pieces_ref, out_ref, grad_ref, buf, small, sems):
    _, chip = place()
    count, heads, width = base_ref.shape
    half = heads // 2
    parts, ranks = lax.axis_size("dp"), lax.axis_size("ctx")
    groups, slot = ranks // 2, width // half
    own = pieces_ref[pl.ds(lax.axis_index("dp") * ranks, ranks)].reshape(groups, 2, 2, width)
    beyond = sum(jnp.where(m > chip, 1.0, 0.0) * own[m, :, 1] for m in range(groups))
    lane, sub = iota((half, width), 1), iota((half, width), 0)
    chosen = [
        jnp.sum(jnp.where(lane == sub * slot, beyond[c : c + 1], 0.0), 1, keepdims=True) for c in range(2)
    ]
    after = jnp.broadcast_to(jnp.concatenate(chosen, 0), (heads, width))
    for t in range(count):
        buf[t] = (base_ref[t] + after * rise_ref[t]).astype(BF16)
    key_copy = pltpu.make_async_copy(buf, out_ref.at[0], sems.at[0])
    key_copy.start()
    total = jnp.sum(pieces_ref[...].reshape(parts * groups, 2, 2, width)[:, :, 0], 0)
    fold = iota((width, slot), 0) % slot == iota((width, slot), 1)
    lines = [jnp.where(lane // slot == sub, total[c : c + 1], 0.0) for c in range(2)]
    small[...] = exact(jnp.concatenate(lines, 0), fold)[:, : width // parts]
    grad_copy = pltpu.make_async_copy(small, grad_ref, sems.at[1])
    grad_copy.start()
    key_copy.wait()
    grad_copy.wait()


def across_chips(total, ends, ranks, reverse):
    step = -1 if reverse else 1

    def shift(value, chips):
        hops = [(i, i + 2 * chips * step) for i in range(ranks) if 0 <= i + 2 * chips * step < ranks]
        return lax.ppermute(value, "ctx", hops)

    value, factor = shift(total, 1), shift(ends, 1)
    reach = 1
    while 2 * reach < ranks:
        value = value + factor * shift(value, reach)
        factor = factor * shift(factor, reach)
        reach *= 2
    return value


def per_device(mesh, queries, keys, values, out_grad, gate_weight, head_bias):
    _, count, heads, width = queries.shape
    parts, ranks = mesh.shape["dp"], mesh.shape["ctx"]
    half = heads // 2
    pair = ranks == 4
    direct = parts == 8
    swap = [(i, i ^ 1) for i in range(ranks)]

    def shape(*dims, dtype=BF16):
        return jax.ShapeDtypeStruct(dims, dtype)

    bias = head_bias.reshape(1, heads)

    quad = shape(4, half, width, count)
    pinned = [
        pltpu.with_memory_space_constraint(x, pltpu.HBM)
        for x in (keys, queries, values, out_grad, gate_weight)
    ]
    keep, send, gate_copy = call(
        split_kernel,
        "split_heads",
        (quad, quad, shape(*gate_weight.shape)),
        pinned,
        [pltpu.VMEM((4, count, heads, width), BF16), pltpu.SemaphoreType.DMA((5,))],
        3.0,
        in_specs=[HBM] * 5,
    )
    if direct:
        nearby = lax.ppermute(gate_weight, "dp", [(i, i ^ 1) for i in range(parts)])
        nearby, send = lax.optimization_barrier((nearby, send))
        two = jnp.stack([gate_copy, nearby])
        gates = [
            lax.ppermute(two, "dp", [(i, i ^ far) for i in range(parts)])
            for far in (2, 6, 4)
        ]
    else:
        gates = [lax.all_gather(gate_weight, "dp", axis=1, tiled=True)]
    recv = lax.ppermute(send, "ctx", swap)
    (products,) = call(
        product_kernel, "products", (shape(half, count, count, dtype=F32),), (keep,), (), 1.0
    )
    *gates, products = lax.optimization_barrier((*gates, products))
    if direct:
        gates = [two, gates[0], gates[2], gates[1]]

    sides = 1 if pair else 2
    lines = pltpu.VMEM((2, heads, count), F32)
    state = shape(sides, half, width, width, dtype=BF16 if pair else F32)
    total, near, rows, gate_full = call(
        functools.partial(gate_kernel, direct, pair),
        "gate_states",
        (state, state, shape(2, heads, count, dtype=F32), shape(2, heads, width, dtype=F32)),
        (*gates, bias, keep, recv),
        [lines],
        1.3,
    )

    attn_shape = shape(sides, 2, half, width, count, dtype=F32)
    mine_shape = shape(sides, half, width, count)
    send_shape = shape(sides, half + 1, width, count)
    slope_shape = shape(2, half, count, dtype=F32)

    def inside(*outs):
        return call(
            functools.partial(inside_kernel, pair),
            "inside_block",
            (attn_shape, *outs),
            (keep, recv, rows, near, products),
            [lines],
            4.0,
        )

    (kappa,) = call(
        kappa_kernel, "kappa", (shape(half, width, dtype=F32),), (keep, recv, rows), (), 0.3
    )
    if pair:
        opposite = [(i, i ^ 2) for i in range(ranks)]
        states = lax.ppermute(total, "ctx", opposite)
        near_shape = shape(1, half, width, width, dtype=F32)
        attn, near, mine_local, send_local, slopes = inside(near_shape, mine_shape, send_shape, slope_shape)
        kappa = lax.ppermute(kappa, "ctx", opposite)
        recv_local = lax.ppermute(send_local, "ctx", swap)
        more = (slopes,)
        local = (mine_local, recv_local)
    else:
        ends = jnp.exp(rows[0, :half, -1] + rows[0, half:, -1])[:, None, None]
        states = jnp.stack(
            [across_chips(total[0], ends, ranks, False), across_chips(total[1], ends, ranks, True)]
        )
        (attn,) = inside()
        kappa = across_chips(kappa, jnp.ones((half, 1), F32), ranks, False)
        more = ()
        local = ()
    mine, send, suffix, pieces = call(
        functools.partial(outside_kernel, pair),
        "outside_block",
        (mine_shape, send_shape, shape(half, count, dtype=F32), shape(parts * ranks, 2, width, dtype=F32)),
        (keep, recv, rows, states, near, attn, kappa, *more),
        [lines],
        1.5,
    )
    pieces = lax.all_to_all(pieces, ("dp", "ctx"), 0, 0, tiled=True)
    recv_out = lax.ppermute(send, "ctx", swap)
    whole = shape(1, count, heads, width)
    plain = shape(count, heads, width, dtype=F32)
    query_grad, base, rise = call(
        functools.partial(merge_kernel, pair),
        "merge_heads",
        (whole, plain, plain),
        (gate_full, suffix, rows, *local, mine, recv_out),
        [pltpu.VMEM((2, heads, count), F32), pltpu.VMEM((2, count * heads, width), F32)],
        2.0,
    )
    key_grad, gate_grad = call(
        last_kernel,
        "key_gradient",
        (whole, shape(heads, width // parts, dtype=F32)),
        (base, rise, pieces),
        [
            pltpu.VMEM((count, heads, width), BF16),
            pltpu.VMEM((heads, width // parts), F32),
            pltpu.SemaphoreType.DMA((2,)),
        ],
        1.0,
        out_specs=(ANY, ANY),
    )
    return query_grad, key_grad, gate_grad


def solution(mesh):
    return jax.shard_map(
        functools.partial(per_device, mesh),
        mesh=mesh,
        in_specs=(
            P("dp", "ctx", None, None),
            P("dp", "ctx", None, None),
            P("dp", "ctx", None, None),
            P("dp", "ctx", None, None),
            P(None, "dp"),
            P(),
        ),
        out_specs=(P("dp", "ctx", None, None), P("dp", "ctx", None, None), P(None, "dp")),
        check_vma=False,
    )
```

```python
import functools

import jax
import jax.numpy as jnp
from jax import lax
from jax.experimental import pallas as pl
from jax.experimental.pallas import tpu as pltpu
from jax.sharding import PartitionSpec as P

F32 = jnp.float32
BF16 = jnp.bfloat16
VMEM = pl.BlockSpec(memory_space=pltpu.VMEM)
ANY = pl.BlockSpec(memory_space=pl.ANY)
HBM = pl.BlockSpec(memory_space=pltpu.HBM)
LIMIT = 24 * 1024 * 1024


def nn(a, b):
    return lax.dot_general(a, b, (((1,), (0,)), ((), ())), preferred_element_type=F32)


def nt(a, b):
    return lax.dot_general(a, b, (((1,), (1,)), ((), ())), preferred_element_type=F32)


def exact(rows, mask):
    count = rows.shape[0]
    parts, rest = [], rows
    for _ in range(3):
        part = rest.astype(BF16)
        parts.append(part)
        rest = rest - part.astype(F32)
    out = nn(jnp.concatenate(parts, 0), jnp.where(mask, 1.0, 0.0).astype(BF16))
    return out[:count] + (out[count : 2 * count] + out[2 * count :])


def iota(shape, dim):
    return lax.broadcasted_iota(jnp.int32, shape, dim)


def place():
    mine = lax.axis_index("ctx")
    return lax.rem(mine, 2), lax.div(mine, 2)


def split_two(rows):
    hi = rows.astype(BF16)
    return hi, (rows - hi.astype(F32)).astype(BF16)


def hi_lo(rows):
    return jnp.concatenate(split_two(rows), 0)


def call(kernel, name, out_shape, operands, scratch=(), micros=1.0, in_specs=None, out_specs=None, limit=LIMIT):
    outs = len(out_shape)
    return pl.pallas_call(
        kernel,
        out_shape=out_shape,
        in_specs=in_specs or [VMEM] * len(operands),
        out_specs=out_specs or (VMEM,) * outs,
        scratch_shapes=list(scratch),
        compiler_params=pltpu.CompilerParams(vmem_limit_bytes=limit),
        cost_estimate=pl.CostEstimate(
            flops=0, bytes_accessed=int(micros * 3_000_000), transcendentals=0
        ),
        name=name,
    )(*operands)


def split_kernel(k_ref, q_ref, v_ref, g_ref, gate_ref, keep_ref, send_ref, copy_ref, buf, sems):
    par, _ = place()
    half = keep_ref.shape[1]
    loads = [
        pltpu.make_async_copy(ref.at[0], buf.at[at], sems.at[at])
        for at, ref in enumerate((k_ref, q_ref, v_ref, g_ref))
    ]
    for load in loads:
        load.start()
    gate = pltpu.make_async_copy(gate_ref, copy_ref, sems.at[len(loads)])
    gate.start()
    for at, load in enumerate(loads):
        load.wait()
        planes = jnp.swapaxes(buf[at], 0, 1)
        for j in range(half):
            first, second = planes[j], planes[half + j]
            if at < 2:
                first, second = first.T, second.T
            keep_ref[at, j] = jnp.where(par == 0, first, second)
            send_ref[at, j] = jnp.where(par == 0, second, first)
    gate.wait()


def scales(rows):
    end = jnp.broadcast_to(rows[:, -1:], rows.shape)
    return jnp.exp(end - rows), jnp.exp(rows), jnp.exp(end)


def whole_gate(direct, gates):
    index = lax.axis_index("dp")
    if not direct:
        return gates[0][...].astype(F32)
    heads, piece = gates[0].shape[1:]
    width = piece * lax.axis_size("dp")
    full = jnp.zeros((heads, width), F32)
    for r, ref in enumerate(gates):
        for low in range(2):
            owner = jnp.bitwise_xor(index, 2 * r + low)
            pick = iota((piece, width), 1) == iota((piece, width), 0) + owner * piece
            full = full + nn(ref[low], jnp.where(pick, 1.0, 0.0).astype(BF16))
    return full


def gate_kernel(direct, pair, chunks, *refs):
    gates, refs = refs[:-chunks - 7], refs[-chunks - 7 :]
    bias_ref, keep_ref, recv_ref, *total_refs, near_ref, rows_ref, gate_ref, scale_ref = refs
    par, chip = place()
    _, half, width, count = keep_ref.shape
    gate_ref[0] = whole_gate(direct, gates)
    same = iota((2 * half, 2 * half), 0) == iota((2 * half, 2 * half), 1)
    spread = jnp.where(same, bias_ref[...].astype(F32), 0.0).astype(BF16)
    gate_ref[1] = nn(spread, jnp.ones((2 * half, width), BF16))
    weights = gate_ref[0, pl.ds(par * half, half), :]
    bias = gate_ref[1, pl.ds(par * half, half), :]
    row, side_of = iota((half, 2 * width), 0), iota((half, 2 * width), 1) // width
    twice = jnp.concatenate([weights, weights], 1)
    logit = jnp.zeros((half, 2 * count), F32)
    for j in range(0, half, 2):
        planes = [ref[0, j : j + 2].reshape(2 * width, count) for ref in (keep_ref, recv_ref)]
        logit = logit + nn(jnp.where(row == j + side_of, twice, 0.0).astype(BF16), jnp.concatenate(planes, 1))
    logit = jnp.concatenate([bias + logit[:, :count], bias + logit[:, count:]], 0)
    decay = -(jnp.maximum(logit, 0.0) + jnp.log1p(jnp.exp(-jnp.abs(logit))))
    cumul = exact(decay, iota((count, count), 0) <= iota((count, count), 1))
    rows_ref[0] = cumul
    rows_ref[1] = -1.0 / (1.0 + jnp.exp(-logit))
    tail, head, ends = scales(cumul)
    scale_ref[0] = tail
    scale_ref[1] = head
    for at, side in enumerate((chip,) if pair else (0, 1)):
        enters = par == side
        for j in range(half):
            states = []
            for rel, ref in enumerate((keep_ref, recv_ref)):
                line = scale_ref[side, rel * half + j : rel * half + j + 1, :]
                scaled = (ref[side, j].astype(F32) * line).astype(BF16)
                states.append(nn(scaled, ref[2 + side, j]))
            own, other = states
            passed = (
                jnp.where(enters, ends[half + j : half + j + 1], 1.0) * own
                + jnp.where(enters, 1.0, ends[j : j + 1]) * other
            )
            size = half // chunks
            total_refs[j // size][at, j % size] = passed.astype(total_refs[0].dtype)
            near_ref[at, j] = jnp.where(enters, own, other).astype(near_ref.dtype)


def weighted_keys(keep_ref, recv_ref, own, other):
    half, count = own.shape
    width = keep_ref.shape[2]
    lhs = jnp.concatenate([hi_lo(own), hi_lo(other)], 1)
    row = iota((2 * half, width), 0) % half
    total = jnp.zeros((2 * half, width), F32)
    for j in range(0, half, 2):
        planes = [ref[0, j : j + 2].reshape(2 * width, count) for ref in (keep_ref, recv_ref)]
        got = nt(lhs, jnp.concatenate(planes, 1))
        total = total + jnp.where(row == j, got[:, :width], 0.0) + jnp.where(row == j + 1, got[:, width:], 0.0)
    return total[:half] + total[half:]


def slope_row(ref, side, j, full):
    sign = jnp.where(side == 0, 1.0, -1.0)
    return sign * jnp.sum(ref[1 - side, j].astype(F32) * full, 0, keepdims=True)


def product_kernel(keep_ref, out_ref):
    for j in range(out_ref.shape[0]):
        out_ref[j] = nt(keep_ref[3, j], keep_ref[2, j])


def kappa_kernel(keep_ref, recv_ref, rows_ref, kappa_ref):
    half = kappa_ref.shape[0]
    kappa_ref[...] = weighted_keys(keep_ref, recv_ref, rows_ref[1, :half, :], rows_ref[1, half:, :])


def inside_kernel(pair, keep_ref, recv_ref, rows_ref, near_ref, product_ref, attn_ref, run_ref, dg_ref, *refs):
    if pair:
        other_ref, mine_ref, send_ref, scale_ref = refs
    else:
        (scale_ref,) = refs
    par, chip = place()
    _, half, width, count = keep_ref.shape
    const = 1.0 / width
    cumul = rows_ref[0]
    columns = cumul.T
    tail, head, _ = scales(cumul)
    scale_ref[0] = tail
    scale_ref[1] = head
    causal = iota((count, count), 0) >= iota((count, count), 1)
    until = jnp.where(iota((count, count), 0) <= iota((count, count), 1), 1.0, 0.0).astype(BF16)
    both = (keep_ref, recv_ref)
    side = chip
    if pair:
        enters = par == 1 - side
        for j in range(half):
            line = jnp.where(
                enters, scale_ref[1 - side, j : j + 1, :], scale_ref[1 - side, half + j : half + j + 1, :]
            )
            left = jnp.where(enters, keep_ref[1 - side, j], recv_ref[1 - side, j])
            right = jnp.where(enters, keep_ref[3 - side, j], recv_ref[3 - side, j])
            other_ref[0, j] = nn((left.astype(F32) * line).astype(BF16), right)
        send_ref[0, half] = jnp.zeros((count, width), BF16)
        send_ref[0, half, : 2 * half] = hi_lo(rows_ref[1, half:, :])
    for rel, ref in enumerate(both):
        block = par if rel == 0 else 1 - par
        slopes = []
        for j in range(half):
            at = rel * half + j
            decay = jnp.exp(jnp.where(causal, columns[:, at : at + 1] - cumul[at : at + 1], -1e30))
            product = product_ref[j] if rel == 0 else nt(ref[3, j], ref[2, j])
            weight = (const * product * decay).astype(BF16)
            query = nt(ref[0, j], weight)
            key = nn(ref[1, j], weight)
            if pair:
                attn_ref[0, rel, j] = jnp.where(side == 0, key, query)
                cross = nt(near_ref[0, j], ref[3 - side, j])
                factor = jnp.where(block == side, 0.0, const) * scale_ref[1 - side, at : at + 1, :]
                full = jnp.where(side == 0, query, key) + factor * cross
                (mine_ref if rel == 0 else send_ref)[0, j] = full.astype(BF16)
                rest = jnp.where(side == 0, key, query)
                slopes.append(slope_row(ref, side, j, full) + slope_row(ref, 1 - side, j, rest))
            else:
                attn_ref[0, rel, j] = query
                attn_ref[1, rel, j] = key
                slopes.append(slope_row(ref, 0, j, query) + slope_row(ref, 1, j, key))
            run = nn(hi_lo(ref[0, j].astype(F32) * rows_ref[1, at : at + 1, :]), until)
            hi, lo = split_two(run[:width] + run[width:])
            run_ref[0, rel, j] = hi
            run_ref[1, rel, j] = lo
        dg_ref[rel] = jnp.concatenate(slopes, 0)


def run_keys(run_ref, own, other):
    half, count = own.shape
    width = run_ref.shape[3]
    lhs = jnp.concatenate([hi_lo(own), hi_lo(other)], 1)
    row = iota((half, width), 0)
    total = jnp.zeros((half, width), F32)
    for j in range(0, half, 2):
        planes = [
            jnp.concatenate([run_ref[p, rel, j : j + 2].reshape(2 * width, count) for rel in range(2)], 1)
            for p in range(2)
        ]
        got = nt(lhs, planes[0])
        got = got[:half] + (got[half:] + nt(lhs[:half], planes[1]))
        total = total + jnp.where(row == j, got[:, :width], 0.0) + jnp.where(row == j + 1, got[:, width:], 0.0)
    return total


def outside_kernel(pair, group, groups, keep_ref, recv_ref, rows_ref, state_ref, near_ref, attn_ref, dg_ref, *refs):
    final = group == groups - 1
    earlier, refs = (refs[:3], refs[3:]) if group else ((), refs)
    if final:
        kappa_ref, run_ref, mine_ref, send_ref, suffix_ref, pieces_ref, scale_ref = refs
    else:
        mine_ref, send_ref, slope_ref, scale_ref = refs
    par, chip = place()
    _, half, width, count = keep_ref.shape
    size = half // groups
    start = group * size
    const = 1.0 / width
    cumul = rows_ref[0]
    tail, head, ends = scales(cumul)
    scale_ref[0] = tail
    scale_ref[1] = head
    sides = mine_ref.shape[0]
    for at in range(sides if group else 0):
        mine_ref[at, :start] = earlier[0][at, :start]
        send_ref[at, :start] = earlier[1][at, :start]
    all_slopes = []
    for rel, ref in enumerate((keep_ref, recv_ref)):
        block = par if rel == 0 else 1 - par
        slopes = dg_ref[rel, start : start + size]
        for at, side in enumerate((1 - chip,) if pair else (0, 1)):
            enters = block == side
            lines = []
            for j in range(start, start + size):
                passed = (1 - rel) * half + j
                come = state_ref[at, j - start].astype(F32)
                moved = ends[passed : passed + 1] * come + near_ref[at, j]
                known = jnp.where(enters, come, moved)
                cross = nt(known.astype(BF16), ref[3 - side, j])
                factor = const * scale_ref[1 - side, rel * half + j : rel * half + j + 1, :]
                lines.append(factor * slope_row(ref, side, j, cross))
                full = attn_ref[at, rel, j] + factor * cross
                (mine_ref if rel == 0 else send_ref)[at, j] = full.astype(BF16)
            slopes = slopes + jnp.concatenate(lines, 0)
        all_slopes.append(slopes)
    if not final:
        for rel in range(2):
            slope_ref[rel] = all_slopes[rel]
        return
    if group:
        all_slopes = [jnp.concatenate([earlier[2][rel], all_slopes[rel]], 0) for rel in range(2)]
    slope = jnp.concatenate(all_slopes, 0)
    sums = jnp.broadcast_to(jnp.sum(slope, 1, keepdims=True), slope.shape)
    first = jnp.where(par == 0, 1.0, 0.0)
    end = iota((half, count), 1) == count - 1
    own = slope[:half] + jnp.where(end, first * sums[half:], 0.0)
    other = slope[half:] + jnp.where(end, (1.0 - first) * sums[:half], 0.0)
    total = sums[:half] + sums[half:]
    before = jnp.where(chip == 1, 1.0, 0.0) if pair else 1.0
    partial = run_keys(run_ref, own, other) + before * (total * kappa_ref[...])
    parts = lax.axis_size("dp")
    ranks = pieces_ref.shape[0] // parts
    piece, slot = width // parts, width // half
    here = iota((half, width), 1) // slot == iota((half, width), 0)
    totals = jnp.sum(jnp.where(here, total, 0.0), 0, keepdims=True)
    for i in range(parts):
        turned = partial if i == 0 else pltpu.roll(partial, width - i * piece, 1)
        turned = pltpu.roll(turned, 0, 1, stride=slot, stride_axis=0)
        line = jnp.sum(jnp.where(here, turned, 0.0), 0, keepdims=True)
        sent = jnp.concatenate([line, totals], 0)
        pieces_ref[pl.ds(i * ranks, ranks)] = jnp.broadcast_to(sent[None], (ranks, 2, width))
    suffix = exact(jnp.concatenate([own, other], 0), iota((count, count), 0) >= iota((count, count), 1))
    suffix_ref[...] = suffix[:half]
    for at in range(sides):
        send_ref[at, half] = jnp.zeros((width, count), BF16)
    if sides == 2:
        send_ref[0, half, : 2 * half] = hi_lo(rows_ref[1, half:, :])
    send_ref[sides - 1, half, : 2 * half] = hi_lo(suffix[half:])


def merge_kernel(pair, gate_ref, suffix_ref, rows_ref, *refs):
    if pair:
        mine0, recv0, mine1, recv1, query_ref, base_ref, rise_ref, line_ref, tmp = refs
        sources = ((mine0, recv0, 0), (mine1, recv1, 0))
    else:
        mine0, recv0, query_ref, base_ref, rise_ref, line_ref, tmp = refs
        sources = ((mine0, recv0, 0), (mine0, recv0, 1))
    par, chip = place()
    _, count, heads, width = query_ref.shape
    half = heads // 2
    for at, (mine, recv, side) in enumerate(sources):
        for j in range(half):
            for ref, base in ((mine, par * half), (recv, (1 - par) * half)):
                tmp[at, pl.ds(base + j, count, stride=heads), :] = ref[side, j].T.astype(F32)
        got = recv[side, half, : 2 * half].astype(F32)
        line_ref[at, pl.ds((1 - par) * half, half), :] = got[:half] + got[half:]
    line_ref[0, pl.ds(par * half, half), :] = rows_ref[1, :half, :]
    line_ref[1, pl.ds(par * half, half), :] = suffix_ref[...]
    first = chip if pair else 0
    query_ref[0] = tmp[first, : count * heads].reshape(count, heads, width).astype(BF16)
    rise = line_ref[0]
    slope = rise * line_ref[1]
    gate = gate_ref[0]
    for t in range(count):
        known = tmp[1 - first, t * heads : (t + 1) * heads, :]
        base_ref[t] = known + slope[:, t : t + 1] * gate
        rise_ref[t] = rise[:, t : t + 1] * gate


def last_kernel(base_ref, rise_ref, pieces_ref, out_ref, grad_ref, buf, small, sems):
    _, chip = place()
    count, heads, width = base_ref.shape
    half = heads // 2
    parts, ranks = lax.axis_size("dp"), lax.axis_size("ctx")
    groups, slot = ranks // 2, width // half
    own = pieces_ref[pl.ds(lax.axis_index("dp") * ranks, ranks)].reshape(groups, 2, 2, width)
    beyond = sum(jnp.where(m > chip, 1.0, 0.0) * own[m, :, 1] for m in range(groups))
    lane, sub = iota((half, width), 1), iota((half, width), 0)
    chosen = [
        jnp.sum(jnp.where(lane == sub * slot, beyond[c : c + 1], 0.0), 1, keepdims=True) for c in range(2)
    ]
    after = jnp.broadcast_to(jnp.concatenate(chosen, 0), (heads, width))
    for t in range(count):
        buf[t] = (base_ref[t] + after * rise_ref[t]).astype(BF16)
    key_copy = pltpu.make_async_copy(buf, out_ref.at[0], sems.at[0])
    key_copy.start()
    total = jnp.sum(pieces_ref[...].reshape(parts * groups, 2, 2, width)[:, :, 0], 0)
    fold = iota((width, slot), 0) % slot == iota((width, slot), 1)
    lines = [jnp.where(lane // slot == sub, total[c : c + 1], 0.0) for c in range(2)]
    small[...] = exact(jnp.concatenate(lines, 0), fold)[:, : width // parts]
    grad_copy = pltpu.make_async_copy(small, grad_ref, sems.at[1])
    grad_copy.start()
    key_copy.wait()
    grad_copy.wait()


def across_chips(total, ends, ranks, reverse):
    step = -1 if reverse else 1

    def shift(value, chips):
        hops = [(i, i + 2 * chips * step) for i in range(ranks) if 0 <= i + 2 * chips * step < ranks]
        return lax.ppermute(value, "ctx", hops)

    value, factor = shift(total, 1), shift(ends, 1)
    reach = 1
    while 2 * reach < ranks:
        value = value + factor * shift(value, reach)
        factor = factor * shift(factor, reach)
        reach *= 2
    return value


def per_device(mesh, queries, keys, values, out_grad, gate_weight, head_bias):
    _, count, heads, width = queries.shape
    parts, ranks = mesh.shape["dp"], mesh.shape["ctx"]
    half = heads // 2
    pair = ranks == 4
    direct = parts == 8
    swap = [(i, i ^ 1) for i in range(ranks)]

    def shape(*dims, dtype=BF16):
        return jax.ShapeDtypeStruct(dims, dtype)

    bias = head_bias.reshape(1, heads)

    quad = shape(4, half, width, count)
    pinned = [
        pltpu.with_memory_space_constraint(x, pltpu.HBM)
        for x in (keys, queries, values, out_grad, gate_weight)
    ]
    keep, send, gate_copy = call(
        split_kernel,
        "split_heads",
        (quad, quad, shape(*gate_weight.shape)),
        pinned,
        [pltpu.VMEM((4, count, heads, width), BF16), pltpu.SemaphoreType.DMA((5,))],
        3.0,
        in_specs=[HBM] * 5,
    )
    if direct:
        nearby = lax.ppermute(gate_weight, "dp", [(i, i ^ 1) for i in range(parts)])
        nearby, send = lax.optimization_barrier((nearby, send))
        two = jnp.stack([gate_copy, nearby])
        gates = [
            lax.ppermute(two, "dp", [(i, i ^ far) for i in range(parts)])
            for far in (2, 6, 4)
        ]
    else:
        gates = [lax.all_gather(gate_weight, "dp", axis=1, tiled=True)]
    recv = lax.ppermute(send, "ctx", swap)
    (products,) = call(
        product_kernel, "products", (shape(half, count, count, dtype=F32),), (keep,), (), 1.0
    )
    *gates, products = lax.optimization_barrier((*gates, products))
    if direct:
        gates = [two, gates[0], gates[2], gates[1]]

    sides = 1 if pair else 2
    lines = pltpu.VMEM((2, heads, count), F32)
    state = shape(sides, half, width, width, dtype=BF16 if pair else F32)
    chunks = 1 if pair else 1
    part = shape(sides, half // chunks, width, width, dtype=state.dtype)
    *totals, near, rows, gate_full = call(
        functools.partial(gate_kernel, direct, pair, chunks),
        "gate_states",
        (part,) * chunks + (state, shape(2, heads, count, dtype=F32), shape(2, heads, width, dtype=F32)),
        (*gates, bias, keep, recv),
        [lines],
        1.3,
    )

    attn_shape = shape(sides, 2, half, width, count, dtype=F32)
    mine_shape = shape(sides, half, width, count)
    send_shape = shape(sides, half + 1, width, count)
    run_shape = shape(2, 2, half, width, count)

    def inside(*outs):
        return call(
            functools.partial(inside_kernel, pair),
            "inside_block",
            (attn_shape, run_shape, shape(2, half, count, dtype=F32), *outs),
            (keep, recv, rows, near, products),
            [lines],
            4.0,
        )

    (kappa,) = call(
        kappa_kernel, "kappa", (shape(half, width, dtype=F32),), (keep, recv, rows), (), 0.3
    )
    if pair:
        opposite = [(i, i ^ 2) for i in range(ranks)]
        states = [lax.ppermute(total, "ctx", opposite) for total in totals]
        near_shape = shape(1, half, width, width, dtype=F32)
        attn, runs, slopes, near, mine_local, send_local = inside(near_shape, mine_shape, send_shape)
        kappa = lax.ppermute(kappa, "ctx", opposite)
        recv_local = lax.ppermute(send_local, "ctx", swap)
        local = (mine_local, recv_local)
    else:
        ends = jnp.exp(rows[0, :half, -1] + rows[0, half:, -1])[:, None, None]
        (total,) = totals
        states = [
            jnp.stack([across_chips(total[0], ends, ranks, False), across_chips(total[1], ends, ranks, True)])
        ]
        attn, runs, slopes = inside()
        kappa = across_chips(kappa, jnp.ones((half, 1), F32), ranks, False)
        local = ()
    earlier = ()
    for group, come in enumerate(states):
        final = group == chunks - 1
        outs = (
            (shape(half, count, dtype=F32), shape(parts * ranks, 2, width, dtype=F32))
            if final
            else (shape(2, half // chunks, count, dtype=F32),)
        )
        earlier = call(
            functools.partial(outside_kernel, pair, group, chunks),
            "outside_block",
            (mine_shape, send_shape, *outs),
            (keep, recv, rows, come, near, attn, slopes, *earlier) + ((kappa, runs) if final else ()),
            [lines],
            1.0,
        )
    mine, send, suffix, pieces = earlier
    pieces = lax.all_to_all(pieces, ("dp", "ctx"), 0, 0, tiled=True)
    recv_out = lax.ppermute(send, "ctx", swap)
    whole = shape(1, count, heads, width)
    plain = shape(count, heads, width, dtype=F32)
    query_grad, base, rise = call(
        functools.partial(merge_kernel, pair),
        "merge_heads",
        (whole, plain, plain),
        (gate_full, suffix, rows, *local, mine, recv_out),
        [pltpu.VMEM((2, heads, count), F32), pltpu.VMEM((2, (count + 1) * heads, width), F32)],
        2.0,
    )
    key_grad, gate_grad = call(
        last_kernel,
        "key_gradient",
        (whole, shape(heads, width // parts, dtype=F32)),
        (base, rise, pieces),
        [
            pltpu.VMEM((count, heads, width), BF16),
            pltpu.VMEM((heads, width // parts), F32),
            pltpu.SemaphoreType.DMA((2,)),
        ],
        1.0,
        out_specs=(ANY, ANY),
    )
    return query_grad, key_grad, gate_grad


def solution(mesh):
    return jax.shard_map(
        functools.partial(per_device, mesh),
        mesh=mesh,
        in_specs=(
            P("dp", "ctx", None, None),
            P("dp", "ctx", None, None),
            P("dp", "ctx", None, None),
            P("dp", "ctx", None, None),
            P(None, "dp"),
            P(),
        ),
        out_specs=(P("dp", "ctx", None, None), P("dp", "ctx", None, None), P(None, "dp")),
        check_vma=False,
    )
```

```python
import functools

import jax
import jax.numpy as jnp
from jax import lax
from jax.experimental import pallas as pl
from jax.experimental.pallas import tpu as pltpu
from jax.sharding import PartitionSpec as P

F32 = jnp.float32
BF16 = jnp.bfloat16
VMEM = pl.BlockSpec(memory_space=pltpu.VMEM)
ANY = pl.BlockSpec(memory_space=pl.ANY)
HBM = pl.BlockSpec(memory_space=pltpu.HBM)
LIMIT = 24 * 1024 * 1024


def nn(a, b):
    return lax.dot_general(a, b, (((1,), (0,)), ((), ())), preferred_element_type=F32)


def nt(a, b):
    return lax.dot_general(a, b, (((1,), (1,)), ((), ())), preferred_element_type=F32)


def exact(rows, mask):
    count = rows.shape[0]
    parts, rest = [], rows
    for _ in range(3):
        part = rest.astype(BF16)
        parts.append(part)
        rest = rest - part.astype(F32)
    out = nn(jnp.concatenate(parts, 0), jnp.where(mask, 1.0, 0.0).astype(BF16))
    return out[:count] + (out[count : 2 * count] + out[2 * count :])


def iota(shape, dim):
    return lax.broadcasted_iota(jnp.int32, shape, dim)


def place():
    mine = lax.axis_index("ctx")
    return lax.rem(mine, 2), lax.div(mine, 2)


def split_two(rows):
    hi = rows.astype(BF16)
    return hi, (rows - hi.astype(F32)).astype(BF16)


def hi_lo(rows):
    return jnp.concatenate(split_two(rows), 0)


def call(kernel, name, out_shape, operands, scratch=(), micros=1.0, in_specs=None, out_specs=None, limit=LIMIT):
    outs = len(out_shape)
    return pl.pallas_call(
        kernel,
        out_shape=out_shape,
        in_specs=in_specs or [VMEM] * len(operands),
        out_specs=out_specs or (VMEM,) * outs,
        scratch_shapes=list(scratch),
        compiler_params=pltpu.CompilerParams(vmem_limit_bytes=limit),
        cost_estimate=pl.CostEstimate(
            flops=0, bytes_accessed=int(micros * 3_000_000), transcendentals=0
        ),
        name=name,
    )(*operands)


def split_kernel(k_ref, q_ref, v_ref, g_ref, gate_ref, keep_ref, send_ref, copy_ref, buf, sems):
    par, _ = place()
    half = keep_ref.shape[1]
    loads = [
        pltpu.make_async_copy(ref.at[0], buf.at[at], sems.at[at])
        for at, ref in enumerate((k_ref, q_ref, v_ref, g_ref))
    ]
    for load in loads:
        load.start()
    gate = pltpu.make_async_copy(gate_ref, copy_ref, sems.at[len(loads)])
    gate.start()
    for at, load in enumerate(loads):
        load.wait()
        planes = jnp.swapaxes(buf[at], 0, 1)
        for j in range(half):
            first, second = planes[j], planes[half + j]
            if at < 2:
                first, second = first.T, second.T
            keep_ref[at, j] = jnp.where(par == 0, first, second)
            send_ref[at, j] = jnp.where(par == 0, second, first)
    gate.wait()


def scales(rows):
    end = jnp.broadcast_to(rows[:, -1:], rows.shape)
    return jnp.exp(end - rows), jnp.exp(rows), jnp.exp(end)


def whole_gate(direct, gates):
    index = lax.axis_index("dp")
    if not direct:
        return gates[0][...].astype(F32)
    heads, piece = gates[0].shape[1:]
    width = piece * lax.axis_size("dp")
    full = jnp.zeros((heads, width), F32)
    for r, ref in enumerate(gates):
        for low in range(2):
            owner = jnp.bitwise_xor(index, 2 * r + low)
            pick = iota((piece, width), 1) == iota((piece, width), 0) + owner * piece
            full = full + nn(ref[low], jnp.where(pick, 1.0, 0.0).astype(BF16))
    return full


def gate_kernel(direct, pair, chunks, *refs):
    gates, refs = refs[:-chunks - 7], refs[-chunks - 7 :]
    bias_ref, keep_ref, recv_ref, *total_refs, near_ref, rows_ref, gate_ref, scale_ref = refs
    par, chip = place()
    _, half, width, count = keep_ref.shape
    gate_ref[0] = whole_gate(direct, gates)
    same = iota((2 * half, 2 * half), 0) == iota((2 * half, 2 * half), 1)
    spread = jnp.where(same, bias_ref[...].astype(F32), 0.0).astype(BF16)
    gate_ref[1] = nn(spread, jnp.ones((2 * half, width), BF16))
    weights = gate_ref[0, pl.ds(par * half, half), :]
    bias = gate_ref[1, pl.ds(par * half, half), :]
    row, side_of = iota((half, 2 * width), 0), iota((half, 2 * width), 1) // width
    twice = jnp.concatenate([weights, weights], 1)
    logit = jnp.zeros((half, 2 * count), F32)
    for j in range(0, half, 2):
        planes = [ref[0, j : j + 2].reshape(2 * width, count) for ref in (keep_ref, recv_ref)]
        logit = logit + nn(jnp.where(row == j + side_of, twice, 0.0).astype(BF16), jnp.concatenate(planes, 1))
    logit = jnp.concatenate([bias + logit[:, :count], bias + logit[:, count:]], 0)
    decay = -(jnp.maximum(logit, 0.0) + jnp.log1p(jnp.exp(-jnp.abs(logit))))
    cumul = exact(decay, iota((count, count), 0) <= iota((count, count), 1))
    rows_ref[0] = cumul
    rows_ref[1] = -1.0 / (1.0 + jnp.exp(-logit))
    tail, head, ends = scales(cumul)
    scale_ref[0] = tail
    scale_ref[1] = head
    for at, side in enumerate((chip,) if pair else (0, 1)):
        enters = par == side
        for j in range(half):
            states = []
            for rel, ref in enumerate((keep_ref, recv_ref)):
                line = scale_ref[side, rel * half + j : rel * half + j + 1, :]
                scaled = (ref[side, j].astype(F32) * line).astype(BF16)
                states.append(nn(scaled, ref[2 + side, j]))
            own, other = states
            passed = (
                jnp.where(enters, ends[half + j : half + j + 1], 1.0) * own
                + jnp.where(enters, 1.0, ends[j : j + 1]) * other
            )
            size = half // chunks
            total_refs[j // size][at, j % size] = passed.astype(total_refs[0].dtype)
            near_ref[at, j] = jnp.where(enters, own, other).astype(near_ref.dtype)


def weighted_keys(keep_ref, recv_ref, own, other):
    half, count = own.shape
    width = keep_ref.shape[2]
    lhs = jnp.concatenate([hi_lo(own), hi_lo(other)], 1)
    row = iota((2 * half, width), 0) % half
    total = jnp.zeros((2 * half, width), F32)
    for j in range(0, half, 2):
        planes = [ref[0, j : j + 2].reshape(2 * width, count) for ref in (keep_ref, recv_ref)]
        got = nt(lhs, jnp.concatenate(planes, 1))
        total = total + jnp.where(row == j, got[:, :width], 0.0) + jnp.where(row == j + 1, got[:, width:], 0.0)
    return total[:half] + total[half:]


def slope_row(ref, side, j, full):
    sign = jnp.where(side == 0, 1.0, -1.0)
    return sign * jnp.sum(ref[1 - side, j].astype(F32) * full, 0, keepdims=True)


def product_kernel(keep_ref, out_ref):
    for j in range(out_ref.shape[0]):
        out_ref[j] = nt(keep_ref[3, j], keep_ref[2, j])


def kappa_kernel(keep_ref, recv_ref, rows_ref, kappa_ref):
    half = kappa_ref.shape[0]
    kappa_ref[...] = weighted_keys(keep_ref, recv_ref, rows_ref[1, :half, :], rows_ref[1, half:, :])


def inside_kernel(pair, keep_ref, recv_ref, rows_ref, near_ref, product_ref, attn_ref, run_ref, dg_ref, *refs):
    if pair:
        other_ref, mine_ref, send_ref, scale_ref = refs
    else:
        (scale_ref,) = refs
    par, chip = place()
    _, half, width, count = keep_ref.shape
    const = 1.0 / width
    cumul = rows_ref[0]
    columns = cumul.T
    tail, head, _ = scales(cumul)
    scale_ref[0] = tail
    scale_ref[1] = head
    causal = iota((count, count), 0) >= iota((count, count), 1)
    until = jnp.where(causal, 1.0, 0.0).astype(BF16)
    both = (keep_ref, recv_ref)
    side = chip
    if pair:
        enters = par == 1 - side
        for j in range(half):
            line = jnp.where(
                enters, scale_ref[1 - side, j : j + 1, :], scale_ref[1 - side, half + j : half + j + 1, :]
            )
            left = jnp.where(enters, keep_ref[1 - side, j], recv_ref[1 - side, j])
            right = jnp.where(enters, keep_ref[3 - side, j], recv_ref[3 - side, j])
            other_ref[0, j] = nn((left.astype(F32) * line).astype(BF16), right)
        send_ref[0, half] = jnp.zeros((count, width), BF16)
        send_ref[0, half, : 2 * half] = hi_lo(rows_ref[1, half:, :])
    for rel, ref in enumerate(both):
        block = par if rel == 0 else 1 - par
        slopes = []
        for j in range(half):
            at = rel * half + j
            decay = jnp.exp(jnp.where(causal, columns[:, at : at + 1] - cumul[at : at + 1], -1e30))
            product = product_ref[j] if rel == 0 else nt(ref[3, j], ref[2, j])
            weight = (const * product * decay).astype(BF16)
            query = nt(ref[0, j], weight)
            key = nn(ref[1, j], weight)
            if pair:
                attn_ref[0, rel, j] = jnp.where(side == 0, key, query)
                cross = nt(near_ref[0, j], ref[3 - side, j])
                factor = jnp.where(block == side, 0.0, const) * scale_ref[1 - side, at : at + 1, :]
                full = jnp.where(side == 0, query, key) + factor * cross
                (mine_ref if rel == 0 else send_ref)[0, j] = full.astype(BF16)
                rest = jnp.where(side == 0, key, query)
                slopes.append(slope_row(ref, side, j, full) + slope_row(ref, 1 - side, j, rest))
            else:
                attn_ref[0, rel, j] = query
                attn_ref[1, rel, j] = key
                slopes.append(slope_row(ref, 0, j, query) + slope_row(ref, 1, j, key))
            run = nt(until, hi_lo(ref[0, j].astype(F32) * rows_ref[1, at : at + 1, :]))
            hi, lo = split_two(run[:, :width] + run[:, width:])
            run_ref[0, j, rel * count : (rel + 1) * count] = hi
            run_ref[1, j, rel * count : (rel + 1) * count] = lo
        dg_ref[rel] = jnp.concatenate(slopes, 0)


def run_keys(run_ref, own, other):
    half, count = own.shape
    width = run_ref.shape[3]
    lhs = jnp.concatenate([hi_lo(own), hi_lo(other)], 1)
    row = iota((half, width), 0)
    total = jnp.zeros((half, width), F32)
    for j in range(0, half, 2):
        planes = [jnp.concatenate([run_ref[p, j], run_ref[p, j + 1]], 1) for p in range(2)]
        got = nn(lhs, planes[0])
        got = got[:half] + (got[half:] + nn(lhs[:half], planes[1]))
        total = total + jnp.where(row == j, got[:, :width], 0.0) + jnp.where(row == j + 1, got[:, width:], 0.0)
    return total


def outside_kernel(pair, group, groups, keep_ref, recv_ref, rows_ref, state_ref, near_ref, attn_ref, dg_ref, *refs):
    final = group == groups - 1
    earlier, refs = (refs[:3], refs[3:]) if group else ((), refs)
    if final:
        kappa_ref, run_ref, mine_ref, send_ref, suffix_ref, *total_refs, pieces_ref, scale_ref = refs
    else:
        mine_ref, send_ref, slope_ref, scale_ref = refs
    par, chip = place()
    _, half, width, count = keep_ref.shape
    size = half // groups
    start = group * size
    const = 1.0 / width
    cumul = rows_ref[0]
    tail, head, ends = scales(cumul)
    scale_ref[0] = tail
    scale_ref[1] = head
    sides = mine_ref.shape[0]
    for at in range(sides if group else 0):
        mine_ref[at, :start] = earlier[0][at, :start]
        send_ref[at, :start] = earlier[1][at, :start]
    all_slopes = []
    for rel, ref in enumerate((keep_ref, recv_ref)):
        block = par if rel == 0 else 1 - par
        slopes = dg_ref[rel, start : start + size]
        for at, side in enumerate((1 - chip,) if pair else (0, 1)):
            enters = block == side
            lines = []
            for j in range(start, start + size):
                passed = (1 - rel) * half + j
                come = state_ref[at, j - start].astype(F32)
                moved = ends[passed : passed + 1] * come + near_ref[at, j]
                known = jnp.where(enters, come, moved)
                cross = nt(known.astype(BF16), ref[3 - side, j])
                factor = const * scale_ref[1 - side, rel * half + j : rel * half + j + 1, :]
                lines.append(factor * slope_row(ref, side, j, cross))
                full = attn_ref[at, rel, j] + factor * cross
                (mine_ref if rel == 0 else send_ref)[at, j] = full.astype(BF16)
            slopes = slopes + jnp.concatenate(lines, 0)
        all_slopes.append(slopes)
    if not final:
        for rel in range(2):
            slope_ref[rel] = all_slopes[rel]
        return
    if group:
        all_slopes = [jnp.concatenate([earlier[2][rel], all_slopes[rel]], 0) for rel in range(2)]
    slope = jnp.concatenate(all_slopes, 0)
    sums = jnp.broadcast_to(jnp.sum(slope, 1, keepdims=True), slope.shape)
    first = jnp.where(par == 0, 1.0, 0.0)
    end = iota((half, count), 1) == count - 1
    own = slope[:half] + jnp.where(end, first * sums[half:], 0.0)
    other = slope[half:] + jnp.where(end, (1.0 - first) * sums[:half], 0.0)
    total = sums[:half] + sums[half:]
    before = jnp.where(chip == 1, 1.0, 0.0) if pair else 1.0
    partial = run_keys(run_ref, own, other) + before * (total * kappa_ref[...])
    parts = lax.axis_size("dp")
    ranks = pieces_ref.shape[0] // parts
    piece, slot = width // parts, width // half
    here = iota((half, width), 1) // slot == iota((half, width), 0)
    totals = jnp.sum(jnp.where(here, total, 0.0), 0, keepdims=True)
    for ref in total_refs:
        ref[...] = total
    for i in range(parts):
        turned = partial if i == 0 else pltpu.roll(partial, width - i * piece, 1)
        turned = pltpu.roll(turned, 0, 1, stride=slot, stride_axis=0)
        sent = jnp.sum(jnp.where(here, turned, 0.0), 0, keepdims=True)
        if not pair:
            sent = jnp.concatenate([sent, totals], 0)
        pieces_ref[pl.ds(i * ranks, ranks)] = jnp.broadcast_to(sent[None], (ranks, *sent.shape))
    suffix = exact(jnp.concatenate([own, other], 0), iota((count, count), 0) >= iota((count, count), 1))
    suffix_ref[...] = suffix[:half]
    for at in range(sides):
        send_ref[at, half] = jnp.zeros((width, count), BF16)
    if sides == 2:
        send_ref[0, half, : 2 * half] = hi_lo(rows_ref[1, half:, :])
    send_ref[sides - 1, half, : 2 * half] = hi_lo(suffix[half:])


def merge_kernel(pair, gate_ref, suffix_ref, rows_ref, *refs):
    if pair:
        mine0, recv0, mine1, recv1, query_ref, base_ref, rise_ref, line_ref, tmp = refs
        sources = ((mine0, recv0, 0), (mine1, recv1, 0))
    else:
        mine0, recv0, query_ref, base_ref, rise_ref, line_ref, tmp = refs
        sources = ((mine0, recv0, 0), (mine0, recv0, 1))
    par, chip = place()
    _, count, heads, width = query_ref.shape
    half = heads // 2
    for at, (mine, recv, side) in enumerate(sources):
        for j in range(half):
            for ref, base in ((mine, par * half), (recv, (1 - par) * half)):
                tmp[at, pl.ds(base + j, count, stride=heads), :] = ref[side, j].T.astype(F32)
        got = recv[side, half, : 2 * half].astype(F32)
        line_ref[at, pl.ds((1 - par) * half, half), :] = got[:half] + got[half:]
    line_ref[0, pl.ds(par * half, half), :] = rows_ref[1, :half, :]
    line_ref[1, pl.ds(par * half, half), :] = suffix_ref[...]
    first = chip if pair else 0
    query_ref[0] = tmp[first, : count * heads].reshape(count, heads, width).astype(BF16)
    rise = line_ref[0]
    slope = rise * line_ref[1]
    gate = gate_ref[0]
    for t in range(count):
        known = tmp[1 - first, t * heads : (t + 1) * heads, :]
        base_ref[t] = known + slope[:, t : t + 1] * gate
        rise_ref[t] = rise[:, t : t + 1] * gate


def sum_pieces(pieces_ref, piece, half):
    everyone, rows, width = pieces_ref.shape
    slot = width // half
    here = iota((half, width), 1) // slot == iota((half, width), 0)
    total = jnp.sum(pieces_ref[...].reshape(everyone // 2, 2, rows, width)[:, :, 0], 0)
    fold = iota((width, slot), 0) % slot == iota((width, slot), 1)
    lines = [jnp.where(here, total[c : c + 1], 0.0) for c in range(2)]
    return exact(jnp.concatenate(lines, 0), fold)[:, :piece]


def gate_gradient_kernel(pieces_ref, grad_ref):
    heads, piece = grad_ref.shape
    grad_ref[...] = sum_pieces(pieces_ref, piece, heads // 2)


def key_gradient_kernel(pair, base_ref, rise_ref, *refs):
    par, chip = place()
    count, heads, width = base_ref.shape
    half = heads // 2
    if pair:
        ahead_ref, across_ref, out_ref, buf, line_ref, sems = refs
        line_ref[pl.ds(par * half, half), :] = ahead_ref[...]
        line_ref[pl.ds((1 - par) * half, half), :] = across_ref[...]
        after = jnp.where(chip == 0, 1.0, 0.0) * line_ref[...]
    else:
        pieces_ref, out_ref, buf, sems = refs
        ranks = lax.axis_size("ctx")
        groups, slot = ranks // 2, width // half
        lane, sub = iota((half, width), 1), iota((half, width), 0)
        own = pieces_ref[pl.ds(lax.axis_index("dp") * ranks, ranks)].reshape(groups, 2, 2, width)
        beyond = sum(jnp.where(m > chip, 1.0, 0.0) * own[m, :, 1] for m in range(groups))
        chosen = [
            jnp.sum(jnp.where(lane == sub * slot, beyond[c : c + 1], 0.0), 1, keepdims=True) for c in range(2)
        ]
        after = jnp.broadcast_to(jnp.concatenate(chosen, 0), (heads, width))
    for t in range(count):
        buf[t] = (base_ref[t] + after * rise_ref[t]).astype(BF16)
    copy = pltpu.make_async_copy(buf, out_ref.at[0], sems.at[0])
    copy.start()
    copy.wait()


def across_chips(total, ends, ranks, reverse):
    step = -1 if reverse else 1

    def shift(value, chips):
        hops = [(i, i + 2 * chips * step) for i in range(ranks) if 0 <= i + 2 * chips * step < ranks]
        return lax.ppermute(value, "ctx", hops)

    value, factor = shift(total, 1), shift(ends, 1)
    reach = 1
    while 2 * reach < ranks:
        value = value + factor * shift(value, reach)
        factor = factor * shift(factor, reach)
        reach *= 2
    return value


def per_device(mesh, queries, keys, values, out_grad, gate_weight, head_bias):
    _, count, heads, width = queries.shape
    parts, ranks = mesh.shape["dp"], mesh.shape["ctx"]
    half = heads // 2
    pair = ranks == 4
    direct = parts == 8
    swap = [(i, i ^ 1) for i in range(ranks)]

    def shape(*dims, dtype=BF16):
        return jax.ShapeDtypeStruct(dims, dtype)

    bias = head_bias.reshape(1, heads)

    quad = shape(4, half, width, count)
    pinned = [
        pltpu.with_memory_space_constraint(x, pltpu.HBM)
        for x in (keys, queries, values, out_grad, gate_weight)
    ]
    keep, send, gate_copy = call(
        split_kernel,
        "split_heads",
        (quad, quad, shape(*gate_weight.shape)),
        pinned,
        [pltpu.VMEM((4, count, heads, width), BF16), pltpu.SemaphoreType.DMA((5,))],
        3.0,
        in_specs=[HBM] * 5,
    )
    if direct:
        nearby = lax.ppermute(gate_weight, "dp", [(i, i ^ 1) for i in range(parts)])
        nearby, send = lax.optimization_barrier((nearby, send))
        two = jnp.stack([gate_copy, nearby])
        gates = [
            lax.ppermute(two, "dp", [(i, i ^ far) for i in range(parts)])
            for far in (2, 6, 4)
        ]
    else:
        gates = [lax.all_gather(gate_weight, "dp", axis=1, tiled=True)]
    recv = lax.ppermute(send, "ctx", swap)
    (products,) = call(
        product_kernel, "products", (shape(half, count, count, dtype=F32),), (keep,), (), 1.0
    )
    *gates, products = lax.optimization_barrier((*gates, products))
    if direct:
        gates = [two, gates[0], gates[2], gates[1]]

    sides = 1 if pair else 2
    lines = pltpu.VMEM((2, heads, count), F32)
    state = shape(sides, half, width, width, dtype=BF16 if pair else F32)
    chunks = 1 if pair else 1
    part = shape(sides, half // chunks, width, width, dtype=state.dtype)
    *totals, near, rows, gate_full = call(
        functools.partial(gate_kernel, direct, pair, chunks),
        "gate_states",
        (part,) * chunks + (state, shape(2, heads, count, dtype=F32), shape(2, heads, width, dtype=F32)),
        (*gates, bias, keep, recv),
        [lines],
        1.3,
    )

    attn_shape = shape(sides, 2, half, width, count, dtype=F32)
    mine_shape = shape(sides, half, width, count)
    send_shape = shape(sides, half + 1, width, count)
    run_shape = shape(2, half, 2 * count, width)

    def inside(*outs):
        return call(
            functools.partial(inside_kernel, pair),
            "inside_block",
            (attn_shape, run_shape, shape(2, half, count, dtype=F32), *outs),
            (keep, recv, rows, near, products),
            [lines],
            4.0,
        )

    (kappa,) = call(
        kappa_kernel, "kappa", (shape(half, width, dtype=F32),), (keep, recv, rows), (), 0.3
    )
    if pair:
        opposite = [(i, i ^ 2) for i in range(ranks)]
        states = [lax.ppermute(total, "ctx", opposite) for total in totals]
        near_shape = shape(1, half, width, width, dtype=F32)
        attn, runs, slopes, near, mine_local, send_local = inside(near_shape, mine_shape, send_shape)
        kappa = lax.ppermute(kappa, "ctx", opposite)
        recv_local = lax.ppermute(send_local, "ctx", swap)
        local = (mine_local, recv_local)
    else:
        ends = jnp.exp(rows[0, :half, -1] + rows[0, half:, -1])[:, None, None]
        (total,) = totals
        states = [
            jnp.stack([across_chips(total[0], ends, ranks, False), across_chips(total[1], ends, ranks, True)])
        ]
        attn, runs, slopes = inside()
        kappa = across_chips(kappa, jnp.ones((half, 1), F32), ranks, False)
        local = ()
    earlier = ()
    for group, come in enumerate(states):
        final = group == chunks - 1
        outs = (
            (shape(half, count, dtype=F32),)
            + ((shape(half, width, dtype=F32),) if pair else ())
            + (shape(parts * ranks, 1 if pair else 2, width, dtype=F32),)
            if final
            else (shape(2, half // chunks, count, dtype=F32),)
        )
        earlier = call(
            functools.partial(outside_kernel, pair, group, chunks),
            "outside_block",
            (mine_shape, send_shape, *outs),
            (keep, recv, rows, come, near, attn, slopes, *earlier) + ((kappa, runs) if final else ()),
            [lines],
            1.0,
        )
    mine, send, suffix, *totals, pieces = earlier
    if pair:
        totals = [lax.ppermute(totals[0], "ctx", [(i, i ^ far) for i in range(ranks)]) for far in (2, 3)]
    pieces = lax.all_to_all(pieces, ("dp", "ctx"), 0, 0, tiled=True)
    recv_out = lax.ppermute(send, "ctx", swap)
    whole = shape(1, count, heads, width)
    plain = shape(count, heads, width, dtype=F32)
    query_grad, base, rise = call(
        functools.partial(merge_kernel, pair),
        "merge_heads",
        (whole, plain, plain),
        (gate_full, suffix, rows, *local, mine, recv_out),
        [pltpu.VMEM((2, heads, count), F32), pltpu.VMEM((2, (count + 1) * heads, width), F32)],
        2.0,
    )
    (key_grad,) = call(
        functools.partial(key_gradient_kernel, pair),
        "key_gradient",
        (whole,),
        (base, rise, *(totals if pair else (pieces,))),
        [pltpu.VMEM((count, heads, width), BF16)]
        + ([pltpu.VMEM((heads, width), F32)] if pair else [])
        + [pltpu.SemaphoreType.DMA((1,))],
        1.0,
        out_specs=(ANY,),
    )
    pieces, key_grad = lax.optimization_barrier((pieces, key_grad))
    (gate_grad,) = call(
        gate_gradient_kernel,
        "gate_gradient",
        (shape(heads, width // parts, dtype=F32),),
        (pieces,),
        (),
        0.5,
    )
    return query_grad, key_grad, gate_grad


def solution(mesh):
    return jax.shard_map(
        functools.partial(per_device, mesh),
        mesh=mesh,
        in_specs=(
            P("dp", "ctx", None, None),
            P("dp", "ctx", None, None),
            P("dp", "ctx", None, None),
            P("dp", "ctx", None, None),
            P(None, "dp"),
            P(),
        ),
        out_specs=(P("dp", "ctx", None, None), P("dp", "ctx", None, None), P(None, "dp")),
        check_vma=False,
    )
```

```python
import functools

import jax
import jax.numpy as jnp
from jax import lax
from jax.experimental import pallas as pl
from jax.experimental.pallas import tpu as pltpu
from jax.sharding import PartitionSpec as P

F32 = jnp.float32
BF16 = jnp.bfloat16
VMEM = pl.BlockSpec(memory_space=pltpu.VMEM)
ANY = pl.BlockSpec(memory_space=pl.ANY)
HBM = pl.BlockSpec(memory_space=pltpu.HBM)
LIMIT = 24 * 1024 * 1024


def nn(a, b):
    return lax.dot_general(a, b, (((1,), (0,)), ((), ())), preferred_element_type=F32)


def nt(a, b):
    return lax.dot_general(a, b, (((1,), (1,)), ((), ())), preferred_element_type=F32)


def exact(rows, mask):
    count = rows.shape[0]
    parts, rest = [], rows
    for _ in range(3):
        part = rest.astype(BF16)
        parts.append(part)
        rest = rest - part.astype(F32)
    out = nn(jnp.concatenate(parts, 0), jnp.where(mask, 1.0, 0.0).astype(BF16))
    return out[:count] + (out[count : 2 * count] + out[2 * count :])


def iota(shape, dim):
    return lax.broadcasted_iota(jnp.int32, shape, dim)


def place():
    mine = lax.axis_index("ctx")
    return lax.rem(mine, 2), lax.div(mine, 2)


def split_two(rows):
    hi = rows.astype(BF16)
    return hi, (rows - hi.astype(F32)).astype(BF16)


def hi_lo(rows):
    return jnp.concatenate(split_two(rows), 0)


def call(kernel, name, out_shape, operands, scratch=(), micros=1.0, in_specs=None, out_specs=None, limit=LIMIT):
    outs = len(out_shape)
    return pl.pallas_call(
        kernel,
        out_shape=out_shape,
        in_specs=in_specs or [VMEM] * len(operands),
        out_specs=out_specs or (VMEM,) * outs,
        scratch_shapes=list(scratch),
        compiler_params=pltpu.CompilerParams(vmem_limit_bytes=limit),
        cost_estimate=pl.CostEstimate(
            flops=0, bytes_accessed=int(micros * 3_000_000), transcendentals=0
        ),
        name=name,
    )(*operands)


def split_kernel(k_ref, q_ref, v_ref, g_ref, gate_ref, keep_ref, send_ref, copy_ref, buf, sems):
    par, _ = place()
    half = keep_ref.shape[1]
    loads = [
        pltpu.make_async_copy(ref.at[0], buf.at[at], sems.at[at])
        for at, ref in enumerate((k_ref, q_ref, v_ref, g_ref))
    ]
    for load in loads:
        load.start()
    gate = pltpu.make_async_copy(gate_ref, copy_ref, sems.at[len(loads)])
    gate.start()
    for at, load in enumerate(loads):
        load.wait()
        planes = jnp.swapaxes(buf[at], 0, 1)
        for j in range(half):
            first, second = planes[j], planes[half + j]
            if at < 2:
                first, second = first.T, second.T
            keep_ref[at, j] = jnp.where(par == 0, first, second)
            send_ref[at, j] = jnp.where(par == 0, second, first)
    gate.wait()


def scales(rows):
    end = jnp.broadcast_to(rows[:, -1:], rows.shape)
    return jnp.exp(end - rows), jnp.exp(rows), jnp.exp(end)


def whole_gate(direct, gates):
    index = lax.axis_index("dp")
    if not direct:
        return gates[0][...].astype(F32)
    heads, piece = gates[0].shape[1:]
    width = piece * lax.axis_size("dp")
    full = jnp.zeros((heads, width), F32)
    for r, ref in enumerate(gates):
        for low in range(2):
            owner = jnp.bitwise_xor(index, 2 * r + low)
            pick = iota((piece, width), 1) == iota((piece, width), 0) + owner * piece
            full = full + nn(ref[low], jnp.where(pick, 1.0, 0.0).astype(BF16))
    return full


def gate_kernel(direct, pair, chunks, *refs):
    gates, refs = refs[:-chunks - 7], refs[-chunks - 7 :]
    bias_ref, keep_ref, recv_ref, *total_refs, near_ref, rows_ref, gate_ref, scale_ref = refs
    par, chip = place()
    _, half, width, count = keep_ref.shape
    gate_ref[0] = whole_gate(direct, gates)
    same = iota((2 * half, 2 * half), 0) == iota((2 * half, 2 * half), 1)
    spread = jnp.where(same, bias_ref[...].astype(F32), 0.0).astype(BF16)
    gate_ref[1] = nn(spread, jnp.ones((2 * half, width), BF16))
    weights = gate_ref[0, pl.ds(par * half, half), :]
    bias = gate_ref[1, pl.ds(par * half, half), :]
    row, side_of = iota((half, 2 * width), 0), iota((half, 2 * width), 1) // width
    twice = jnp.concatenate([weights, weights], 1)
    logit = jnp.zeros((half, 2 * count), F32)
    for j in range(0, half, 2):
        planes = [ref[0, j : j + 2].reshape(2 * width, count) for ref in (keep_ref, recv_ref)]
        logit = logit + nn(jnp.where(row == j + side_of, twice, 0.0).astype(BF16), jnp.concatenate(planes, 1))
    logit = jnp.concatenate([bias + logit[:, :count], bias + logit[:, count:]], 0)
    decay = -(jnp.maximum(logit, 0.0) + jnp.log1p(jnp.exp(-jnp.abs(logit))))
    cumul = exact(decay, iota((count, count), 0) <= iota((count, count), 1))
    rows_ref[0] = cumul
    rows_ref[1] = -1.0 / (1.0 + jnp.exp(-logit))
    tail, head, ends = scales(cumul)
    scale_ref[0] = tail
    scale_ref[1] = head
    for at, side in enumerate((chip,) if pair else (0, 1)):
        enters = par == side
        for j in range(half):
            states = []
            for rel, ref in enumerate((keep_ref, recv_ref)):
                line = scale_ref[side, rel * half + j : rel * half + j + 1, :]
                scaled = (ref[side, j].astype(F32) * line).astype(BF16)
                states.append(nn(scaled, ref[2 + side, j]))
            own, other = states
            passed = (
                jnp.where(enters, ends[half + j : half + j + 1], 1.0) * own
                + jnp.where(enters, 1.0, ends[j : j + 1]) * other
            )
            size = half // chunks
            total_refs[j // size][at, j % size] = passed.astype(total_refs[0].dtype)
            near_ref[at, j] = jnp.where(enters, own, other).astype(near_ref.dtype)


def weighted_keys(keep_ref, recv_ref, own, other):
    half, count = own.shape
    width = keep_ref.shape[2]
    lhs = jnp.concatenate([hi_lo(own), hi_lo(other)], 1)
    row = iota((2 * half, width), 0) % half
    total = jnp.zeros((2 * half, width), F32)
    for j in range(0, half, 2):
        planes = [ref[0, j : j + 2].reshape(2 * width, count) for ref in (keep_ref, recv_ref)]
        got = nt(lhs, jnp.concatenate(planes, 1))
        total = total + jnp.where(row == j, got[:, :width], 0.0) + jnp.where(row == j + 1, got[:, width:], 0.0)
    return total[:half] + total[half:]


def slope_row(ref, side, j, full):
    sign = jnp.where(side == 0, 1.0, -1.0)
    return sign * jnp.sum(ref[1 - side, j].astype(F32) * full, 0, keepdims=True)


def product_kernel(keep_ref, out_ref):
    for j in range(out_ref.shape[0]):
        out_ref[j] = nt(keep_ref[3, j], keep_ref[2, j])


def kappa_kernel(keep_ref, recv_ref, rows_ref, kappa_ref):
    half = kappa_ref.shape[0]
    kappa_ref[...] = weighted_keys(keep_ref, recv_ref, rows_ref[1, :half, :], rows_ref[1, half:, :])


def inside_kernel(pair, keep_ref, recv_ref, rows_ref, near_ref, product_ref, attn_ref, run_ref, dg_ref, *refs):
    if pair:
        other_ref, mine_ref, send_ref, scale_ref = refs
    else:
        (scale_ref,) = refs
    par, chip = place()
    _, half, width, count = keep_ref.shape
    const = 1.0 / width
    cumul = rows_ref[0]
    columns = cumul.T
    tail, head, _ = scales(cumul)
    scale_ref[0] = tail
    scale_ref[1] = head
    causal = iota((count, count), 0) >= iota((count, count), 1)
    until = jnp.where(iota((count, count), 0) <= iota((count, count), 1), 1.0, 0.0).astype(BF16)
    both = (keep_ref, recv_ref)
    side = chip
    if pair:
        enters = par == 1 - side
        for j in range(half):
            line = jnp.where(
                enters, scale_ref[1 - side, j : j + 1, :], scale_ref[1 - side, half + j : half + j + 1, :]
            )
            left = jnp.where(enters, keep_ref[1 - side, j], recv_ref[1 - side, j])
            right = jnp.where(enters, keep_ref[3 - side, j], recv_ref[3 - side, j])
            other_ref[0, j] = nn((left.astype(F32) * line).astype(BF16), right)
        send_ref[0, half] = jnp.zeros((count, width), BF16)
        send_ref[0, half, : 2 * half] = hi_lo(rows_ref[1, half:, :])
    for rel, ref in enumerate(both):
        block = par if rel == 0 else 1 - par
        slopes = []
        for j in range(half):
            at = rel * half + j
            decay = jnp.exp(jnp.where(causal, columns[:, at : at + 1] - cumul[at : at + 1], -1e30))
            product = product_ref[j] if rel == 0 else nt(ref[3, j], ref[2, j])
            weight = (const * product * decay).astype(BF16)
            query = nt(ref[0, j], weight)
            key = nn(ref[1, j], weight)
            if pair:
                attn_ref[0, rel, j] = jnp.where(side == 0, key, query)
                cross = nt(near_ref[0, j], ref[3 - side, j])
                factor = jnp.where(block == side, 0.0, const) * scale_ref[1 - side, at : at + 1, :]
                full = jnp.where(side == 0, query, key) + factor * cross
                (mine_ref if rel == 0 else send_ref)[0, j] = full.astype(BF16)
                rest = jnp.where(side == 0, key, query)
                slopes.append(slope_row(ref, side, j, full) + slope_row(ref, 1 - side, j, rest))
            else:
                attn_ref[0, rel, j] = query
                attn_ref[1, rel, j] = key
                slopes.append(slope_row(ref, 0, j, query) + slope_row(ref, 1, j, key))
            run = nn(hi_lo(ref[0, j].astype(F32) * rows_ref[1, at : at + 1, :]), until)
            hi, lo = split_two(run[:width] + run[width:])
            run_ref[0, rel, j] = hi
            run_ref[1, rel, j] = lo
        dg_ref[rel] = jnp.concatenate(slopes, 0)


def run_keys(run_ref, own, other):
    half, count = own.shape
    width = run_ref.shape[3]
    lhs = jnp.concatenate([hi_lo(own), hi_lo(other)], 1)
    row = iota((half, width), 0)
    total = jnp.zeros((half, width), F32)
    for j in range(0, half, 2):
        planes = [
            jnp.concatenate([run_ref[p, rel, j : j + 2].reshape(2 * width, count) for rel in range(2)], 1)
            for p in range(2)
        ]
        got = nt(lhs, planes[0])
        got = got[:half] + (got[half:] + nt(lhs[:half], planes[1]))
        total = total + jnp.where(row == j, got[:, :width], 0.0) + jnp.where(row == j + 1, got[:, width:], 0.0)
    return total


def outside_kernel(pair, group, groups, keep_ref, recv_ref, rows_ref, state_ref, near_ref, attn_ref, dg_ref, *refs):
    final = group == groups - 1
    earlier, refs = (refs[:3], refs[3:]) if group else ((), refs)
    if final:
        kappa_ref, run_ref, mine_ref, send_ref, suffix_ref, *total_refs, pieces_ref, scale_ref = refs
    else:
        mine_ref, send_ref, slope_ref, scale_ref = refs
    par, chip = place()
    _, half, width, count = keep_ref.shape
    size = half // groups
    start = group * size
    const = 1.0 / width
    cumul = rows_ref[0]
    tail, head, ends = scales(cumul)
    scale_ref[0] = tail
    scale_ref[1] = head
    sides = mine_ref.shape[0]
    for at in range(sides if group else 0):
        mine_ref[at, :start] = earlier[0][at, :start]
        send_ref[at, :start] = earlier[1][at, :start]
    all_slopes = []
    for rel, ref in enumerate((keep_ref, recv_ref)):
        block = par if rel == 0 else 1 - par
        slopes = dg_ref[rel, start : start + size]
        for at, side in enumerate((1 - chip,) if pair else (0, 1)):
            enters = block == side
            lines = []
            for j in range(start, start + size):
                passed = (1 - rel) * half + j
                come = state_ref[at, j - start].astype(F32)
                moved = ends[passed : passed + 1] * come + near_ref[at, j]
                known = jnp.where(enters, come, moved)
                cross = nt(known.astype(BF16), ref[3 - side, j])
                factor = const * scale_ref[1 - side, rel * half + j : rel * half + j + 1, :]
                lines.append(factor * slope_row(ref, side, j, cross))
                full = attn_ref[at, rel, j] + factor * cross
                (mine_ref if rel == 0 else send_ref)[at, j] = full.astype(BF16)
            slopes = slopes + jnp.concatenate(lines, 0)
        all_slopes.append(slopes)
    if not final:
        for rel in range(2):
            slope_ref[rel] = all_slopes[rel]
        return
    if group:
        all_slopes = [jnp.concatenate([earlier[2][rel], all_slopes[rel]], 0) for rel in range(2)]
    slope = jnp.concatenate(all_slopes, 0)
    sums = jnp.broadcast_to(jnp.sum(slope, 1, keepdims=True), slope.shape)
    first = jnp.where(par == 0, 1.0, 0.0)
    end = iota((half, count), 1) == count - 1
    own = slope[:half] + jnp.where(end, first * sums[half:], 0.0)
    other = slope[half:] + jnp.where(end, (1.0 - first) * sums[:half], 0.0)
    total = sums[:half] + sums[half:]
    before = jnp.where(chip == 1, 1.0, 0.0) if pair else 1.0
    partial = run_keys(run_ref, own, other) + before * (total * kappa_ref[...])
    parts = lax.axis_size("dp")
    ranks = pieces_ref.shape[0] // parts
    piece, slot = width // parts, width // half
    here = iota((half, width), 1) // slot == iota((half, width), 0)
    totals = jnp.sum(jnp.where(here, total, 0.0), 0, keepdims=True)
    for ref in total_refs:
        ref[...] = total
    for i in range(parts):
        turned = partial if i == 0 else pltpu.roll(partial, width - i * piece, 1)
        turned = pltpu.roll(turned, 0, 1, stride=slot, stride_axis=0)
        sent = jnp.sum(jnp.where(here, turned, 0.0), 0, keepdims=True)
        if not pair:
            sent = jnp.concatenate([sent, totals], 0)
        pieces_ref[pl.ds(i * ranks, ranks)] = jnp.broadcast_to(sent[None], (ranks, *sent.shape))
    suffix = exact(jnp.concatenate([own, other], 0), iota((count, count), 0) >= iota((count, count), 1))
    suffix_ref[...] = suffix[:half]
    for at in range(sides):
        send_ref[at, half] = jnp.zeros((width, count), BF16)
    if sides == 2:
        send_ref[0, half, : 2 * half] = hi_lo(rows_ref[1, half:, :])
    send_ref[sides - 1, half, : 2 * half] = hi_lo(suffix[half:])


def merge_kernel(pair, gate_ref, suffix_ref, rows_ref, *refs):
    if pair:
        mine0, recv0, mine1, recv1, query_ref, base_ref, rise_ref, line_ref, tmp = refs
        sources = ((mine0, recv0, 0), (mine1, recv1, 0))
    else:
        mine0, recv0, query_ref, base_ref, rise_ref, line_ref, tmp = refs
        sources = ((mine0, recv0, 0), (mine0, recv0, 1))
    par, chip = place()
    _, count, heads, width = query_ref.shape
    half = heads // 2
    for at, (mine, recv, side) in enumerate(sources):
        for j in range(half):
            for ref, base in ((mine, par * half), (recv, (1 - par) * half)):
                tmp[at, pl.ds(base + j, count, stride=heads), :] = ref[side, j].T.astype(F32)
        got = recv[side, half, : 2 * half].astype(F32)
        line_ref[at, pl.ds((1 - par) * half, half), :] = got[:half] + got[half:]
    line_ref[0, pl.ds(par * half, half), :] = rows_ref[1, :half, :]
    line_ref[1, pl.ds(par * half, half), :] = suffix_ref[...]
    first = chip if pair else 0
    query_ref[0] = tmp[first, : count * heads].reshape(count, heads, width).astype(BF16)
    rise = line_ref[0]
    slope = rise * line_ref[1]
    gate = gate_ref[0]
    for t in range(count):
        known = tmp[1 - first, t * heads : (t + 1) * heads, :]
        base_ref[t] = known + slope[:, t : t + 1] * gate
        rise_ref[t] = rise[:, t : t + 1] * gate


def sum_pieces(pieces_ref, piece, half):
    everyone, rows, width = pieces_ref.shape
    slot = width // half
    here = iota((half, width), 1) // slot == iota((half, width), 0)
    total = jnp.sum(pieces_ref[...].reshape(everyone // 2, 2, rows, width)[:, :, 0], 0)
    fold = iota((width, slot), 0) % slot == iota((width, slot), 1)
    lines = [jnp.where(here, total[c : c + 1], 0.0) for c in range(2)]
    return exact(jnp.concatenate(lines, 0), fold)[:, :piece]


def gate_gradient_kernel(pieces_ref, grad_ref):
    heads, piece = grad_ref.shape
    grad_ref[...] = sum_pieces(pieces_ref, piece, heads // 2)


def key_gradient_kernel(pair, base_ref, rise_ref, *refs):
    par, chip = place()
    count, heads, width = base_ref.shape
    half = heads // 2
    if pair:
        ahead_ref, across_ref, out_ref, buf, line_ref, sems = refs
        line_ref[pl.ds(par * half, half), :] = ahead_ref[...]
        line_ref[pl.ds((1 - par) * half, half), :] = across_ref[...]
        after = jnp.where(chip == 0, 1.0, 0.0) * line_ref[...]
    else:
        pieces_ref, out_ref, buf, sems = refs
        ranks = lax.axis_size("ctx")
        groups, slot = ranks // 2, width // half
        lane, sub = iota((half, width), 1), iota((half, width), 0)
        own = pieces_ref[pl.ds(lax.axis_index("dp") * ranks, ranks)].reshape(groups, 2, 2, width)
        beyond = sum(jnp.where(m > chip, 1.0, 0.0) * own[m, :, 1] for m in range(groups))
        chosen = [
            jnp.sum(jnp.where(lane == sub * slot, beyond[c : c + 1], 0.0), 1, keepdims=True) for c in range(2)
        ]
        after = jnp.broadcast_to(jnp.concatenate(chosen, 0), (heads, width))
    for t in range(count):
        buf[t] = (base_ref[t] + after * rise_ref[t]).astype(BF16)
    copy = pltpu.make_async_copy(buf, out_ref.at[0], sems.at[0])
    copy.start()
    copy.wait()


def across_chips(total, ends, ranks, reverse):
    step = -1 if reverse else 1

    def shift(value, chips):
        hops = [(i, i + 2 * chips * step) for i in range(ranks) if 0 <= i + 2 * chips * step < ranks]
        return lax.ppermute(value, "ctx", hops)

    value, factor = shift(total, 1), shift(ends, 1)
    reach = 1
    while 2 * reach < ranks:
        value = value + factor * shift(value, reach)
        factor = factor * shift(factor, reach)
        reach *= 2
    return value


def per_device(mesh, queries, keys, values, out_grad, gate_weight, head_bias):
    _, count, heads, width = queries.shape
    parts, ranks = mesh.shape["dp"], mesh.shape["ctx"]
    half = heads // 2
    pair = ranks == 4
    direct = parts == 8
    swap = [(i, i ^ 1) for i in range(ranks)]

    def shape(*dims, dtype=BF16):
        return jax.ShapeDtypeStruct(dims, dtype)

    bias = head_bias.reshape(1, heads)

    quad = shape(4, half, width, count)
    pinned = [
        pltpu.with_memory_space_constraint(x, pltpu.HBM)
        for x in (keys, queries, values, out_grad, gate_weight)
    ]
    keep, send, gate_copy = call(
        split_kernel,
        "split_heads",
        (quad, quad, shape(*gate_weight.shape)),
        pinned,
        [pltpu.VMEM((4, count, heads, width), BF16), pltpu.SemaphoreType.DMA((5,))],
        3.0,
        in_specs=[HBM] * 5,
    )
    if direct:
        nearby = lax.ppermute(gate_weight, "dp", [(i, i ^ 1) for i in range(parts)])
        nearby, send = lax.optimization_barrier((nearby, send))
        two = jnp.stack([gate_copy, nearby])
        gates = [
            lax.ppermute(two, "dp", [(i, i ^ far) for i in range(parts)])
            for far in (4, 2, 6)
        ]
    else:
        gates = [lax.all_gather(gate_weight, "dp", axis=1, tiled=True)]
    recv = lax.ppermute(send, "ctx", swap)
    (products,) = call(
        product_kernel, "products", (shape(half, count, count, dtype=F32),), (keep,), (), 1.0
    )
    *gates, products = lax.optimization_barrier((*gates, products))
    if direct:
        gates = [two, gates[1], gates[0], gates[2]]

    sides = 1 if pair else 2
    lines = pltpu.VMEM((2, heads, count), F32)
    state = shape(sides, half, width, width, dtype=BF16 if pair else F32)
    chunks = 1 if pair else 1
    part = shape(sides, half // chunks, width, width, dtype=state.dtype)
    *totals, near, rows, gate_full = call(
        functools.partial(gate_kernel, direct, pair, chunks),
        "gate_states",
        (part,) * chunks + (state, shape(2, heads, count, dtype=F32), shape(2, heads, width, dtype=F32)),
        (*gates, bias, keep, recv),
        [lines],
        1.3,
    )

    attn_shape = shape(sides, 2, half, width, count, dtype=F32)
    mine_shape = shape(sides, half, width, count)
    send_shape = shape(sides, half + 1, width, count)
    run_shape = shape(2, 2, half, width, count)

    def inside(*outs):
        return call(
            functools.partial(inside_kernel, pair),
            "inside_block",
            (attn_shape, run_shape, shape(2, half, count, dtype=F32), *outs),
            (keep, recv, rows, near, products),
            [lines],
            4.0,
        )

    (kappa,) = call(
        kappa_kernel, "kappa", (shape(half, width, dtype=F32),), (keep, recv, rows), (), 0.3
    )
    if pair:
        opposite = [(i, i ^ 2) for i in range(ranks)]
        states = [lax.ppermute(total, "ctx", opposite) for total in totals]
        near_shape = shape(1, half, width, width, dtype=F32)
        attn, runs, slopes, near, mine_local, send_local = inside(near_shape, mine_shape, send_shape)
        kappa = lax.ppermute(kappa, "ctx", opposite)
        recv_local = lax.ppermute(send_local, "ctx", swap)
        local = (mine_local, recv_local)
    else:
        ends = jnp.exp(rows[0, :half, -1] + rows[0, half:, -1])[:, None, None]
        (total,) = totals
        states = [
            jnp.stack([across_chips(total[0], ends, ranks, False), across_chips(total[1], ends, ranks, True)])
        ]
        attn, runs, slopes = inside()
        kappa = across_chips(kappa, jnp.ones((half, 1), F32), ranks, False)
        local = ()
    earlier = ()
    for group, come in enumerate(states):
        final = group == chunks - 1
        outs = (
            (shape(half, count, dtype=F32),)
            + ((shape(half, width, dtype=F32),) if pair else ())
            + (shape(parts * ranks, 1 if pair else 2, width, dtype=F32),)
            if final
            else (shape(2, half // chunks, count, dtype=F32),)
        )
        earlier = call(
            functools.partial(outside_kernel, pair, group, chunks),
            "outside_block",
            (mine_shape, send_shape, *outs),
            (keep, recv, rows, come, near, attn, slopes, *earlier) + ((kappa, runs) if final else ()),
            [lines],
            1.0,
        )
    mine, send, suffix, *totals, pieces = earlier
    if pair:
        totals = [lax.ppermute(totals[0], "ctx", [(i, i ^ far) for i in range(ranks)]) for far in (2, 3)]
    pieces = lax.all_to_all(pieces, ("dp", "ctx"), 0, 0, tiled=True)
    recv_out = lax.ppermute(send, "ctx", swap)
    whole = shape(1, count, heads, width)
    plain = shape(count, heads, width, dtype=F32)
    query_grad, base, rise = call(
        functools.partial(merge_kernel, pair),
        "merge_heads",
        (whole, plain, plain),
        (gate_full, suffix, rows, *local, mine, recv_out),
        [pltpu.VMEM((2, heads, count), F32), pltpu.VMEM((2, (count + 1) * heads, width), F32)],
        2.0,
    )
    (key_grad,) = call(
        functools.partial(key_gradient_kernel, pair),
        "key_gradient",
        (whole,),
        (base, rise, *(totals if pair else (pieces,))),
        [pltpu.VMEM((count, heads, width), BF16)]
        + ([pltpu.VMEM((heads, width), F32)] if pair else [])
        + [pltpu.SemaphoreType.DMA((1,))],
        1.0,
        out_specs=(ANY,),
    )
    pieces, key_grad = lax.optimization_barrier((pieces, key_grad))
    (gate_grad,) = call(
        gate_gradient_kernel,
        "gate_gradient",
        (shape(heads, width // parts, dtype=F32),),
        (pieces,),
        (),
        0.5,
    )
    return query_grad, key_grad, gate_grad


def solution(mesh):
    return jax.shard_map(
        functools.partial(per_device, mesh),
        mesh=mesh,
        in_specs=(
            P("dp", "ctx", None, None),
            P("dp", "ctx", None, None),
            P("dp", "ctx", None, None),
            P("dp", "ctx", None, None),
            P(None, "dp"),
            P(),
        ),
        out_specs=(P("dp", "ctx", None, None), P("dp", "ctx", None, None), P(None, "dp")),
        check_vma=False,
    )
```
